256 devices in a mesh: tp: 8 (over x, core), cp: 32 (over z, y).
Axes of the slice: x: 4, y: 4, z: 8, core: 2. Of those that a mesh axis runs over, the one named last changes fastest.
Arguments:
- query: bfloat16 [4096, 128, 576], P('cp', 'tp'), may hold values from -36 to 36
- latent: bfloat16 [4096, 576], P('cp'), may hold values from -6 to 6
- grad_out: bfloat16 [4096, 128, 512], P('cp', 'tp'), may hold values from -24 to 24
- ancestors: int32 [32, 3], P('cp'), may hold values from -1 to 30, as said below
- parents: int32 [4096], P('cp'), may hold values from -1 to 126, as said below
Outputs:
- d_query: bfloat16 [4096, 128, 576], P('cp', 'tp')
- d_latent: bfloat16 [4096, 576], P('cp')
The draws below stay inside these ranges and needn't reach their ends.
Inputs may be any that keep to these rules, and one draw needn't show every extreme that they name: `ancestors`: an entry that is not -1 names a block b - t with 1 <= t <= 3; the entries of one block differ from each other. Every block from 3 on whose id is a multiple of 3 lists 3 blocks. The last block lists the block before it. `parents`: the first row of each block is its root (-1); every other row names an earlier row of its own block; the last row of each block names the row before it.
All inputs are finite; a program needn't handle non-finite values.
Results may differ from the reference program's by a relative error of at most 0.01.
Values may be sent and summed in bfloat16 or wider, within the bound.
No kernel may reach another device: no remote copies, remote signals or barrier semaphores. Data moves between devices by JAX's collectives and lax.ppermute only.
A program may use at most 64 MiB of HBM per device.

```python
import jax
import jax.numpy as jnp
from jax import lax

HEADS = 128
LAT = 512
ROPE = 64
BS = 128
BLK_DEV = 1
ANC = 3
REACH = 3
NBLK = 32
ROWS = 4096


def shared_keys(key):
    return jnp.clip(jax.random.normal(key, (ROWS, LAT + ROPE), jnp.float32), -6.0, 6.0)


def draw_latent(key, part):
    base_keys = shared_keys(key)
    return base_keys.astype(jnp.bfloat16)


def draw_query(key, part):
    key = jax.random.fold_in(key, 7)
    values = jnp.clip(jax.random.normal(key, (ROWS, HEADS, LAT + ROPE), jnp.float32), -6.0, 6.0)
    return values.astype(jnp.bfloat16)


def draw_ancestors(key, part):
    key = jax.random.fold_in(key, 3)
    order_key, count_key = jax.random.split(key)
    window = REACH * BLK_DEV
    block_index = jnp.arange(NBLK, dtype=jnp.int32)
    ranked = jax.random.randint(order_key, (NBLK, window), 0, 1 << 20) * window + jnp.arange(window, dtype=jnp.int32)[None, :]
    forced = (block_index[:, None] == NBLK - 1) & (jnp.arange(window, dtype=jnp.int32)[None, :] == 0)
    ranked = jnp.where(forced, -1, ranked)
    order = jnp.argsort(ranked, axis=1, stable=True)[:, :ANC].astype(jnp.int32)
    offsets = order + 1
    counts = jax.random.randint(count_key, (NBLK,), 1, ANC + 1)
    counts = jnp.where(block_index % 3 == 0, ANC, counts)
    listed = block_index[:, None] - offsets
    keep = (jnp.arange(ANC, dtype=jnp.int32)[None, :] < counts[:, None]) & (listed >= 0)
    return jnp.where(keep, listed, -1).astype(jnp.int32)


def draw_parents(key, part):
    key = jax.random.fold_in(key, 5)
    local_row = jnp.arange(ROWS, dtype=jnp.int32) % BS
    picks = jax.random.randint(key, (ROWS,), 0, jnp.maximum(local_row, 1))
    picks = jnp.where(local_row == BS - 1, BS - 2, picks)
    return jnp.where(local_row == 0, -1, picks).astype(jnp.int32)


def block_levels(rng, extent, shards, smallest, top_value):
    level, own = 1.0, jax.random.fold_in(rng, 6)
    for axis_at, parts in shards:
        heights = jnp.exp(jax.random.uniform(jax.random.fold_in(own, axis_at), (parts,), jnp.float32, smallest / len(shards), top_value / len(shards)))
        level = level * jnp.repeat(heights, extent[axis_at] // parts).reshape([-1 if axis == axis_at else 1 for axis in range(len(extent))])
    return level


def gaussian(rng, shape, scale, limit, cuts=(), kind=jnp.bfloat16):
    values = scale * jax.random.normal(rng, shape, jnp.float32)
    if cuts:
        values = values * block_levels(rng, shape, cuts, -0.22, 0.18)
    return jnp.clip(values, -limit, limit).astype(kind)


def setup_inputs(seed: int = 0) -> dict:
    splits = jax.random.split(jax.random.key(seed), 6)
    return {
        "query": draw_query(jax.random.fold_in(splits[5], 71), 0),
        "latent": draw_latent(jax.random.fold_in(splits[5], 71), 0),
        "grad_out": gaussian(splits[2], (ROWS, HEADS, LAT), 4.0, 24.0, ((0, 32), (1, 8))),
        "ancestors": draw_ancestors(jax.random.fold_in(splits[5], 71), 0),
        "parents": draw_parents(jax.random.fold_in(splits[5], 71), 0),
    }


score_scale = 192.0 ** -0.5
rope_base = 10000.0


def tree_positions(ancestors, parents):
    blocks = ancestors.shape[0]
    parent_rows = parents.reshape(blocks, BS)
    row_index = jnp.arange(BS, dtype=jnp.int32)
    linked = (row_index[None, None, :] == parent_rows[:, :, None]) | (row_index[None, None, :] == row_index[None, :, None])
    closure = linked.astype(jnp.float32)
    for sweep in range(max(1, (BS - 1).bit_length())):
        closure = jnp.minimum(jnp.einsum("bij,bjk->bik", closure, closure, precision=lax.Precision.HIGHEST), 1.0)
    tree_depth = jnp.sum(closure, axis=2) - 1.0
    list_count = jnp.sum((ancestors >= 0).astype(jnp.float32), axis=1)
    positions = BS * list_count[:, None] + tree_depth
    return closure, positions.reshape(-1)


def rope_tables(positions):
    half_width = ROPE // 2
    frequency = rope_base ** (-2.0 * jnp.arange(half_width, dtype=jnp.float32) / ROPE)
    angles = positions[:, None] * frequency[None, :]
    return jnp.cos(angles), jnp.sin(angles)


def rotate(values, cosine_table, sine_table):
    half_width = values.shape[-1] // 2
    first_half = values[..., :half_width]
    second_half = values[..., half_width:]
    return jnp.concatenate([first_half * cosine_table - second_half * sine_table, first_half * sine_table + second_half * cosine_table], axis=-1)


def unrotate(values, cosine_table, sine_table):
    half_width = values.shape[-1] // 2
    first_half = values[..., :half_width]
    second_half = values[..., half_width:]
    return jnp.concatenate([first_half * cosine_table + second_half * sine_table, second_half * cosine_table - first_half * sine_table], axis=-1)


def with_rope(values, cosine_table, sine_table):
    plain = values[..., :LAT].astype(jnp.float32)
    turned = rotate(values[..., LAT:].astype(jnp.float32), cosine_table, sine_table)
    return jnp.concatenate([plain, turned], axis=-1)


def reference(query, latent, grad_out, ancestors, parents):
    closure, positions = tree_positions(ancestors, parents)
    cosine_table, sine_table = rope_tables(positions)
    query_rot = with_rope(query, cosine_table[:, None, :], sine_table[:, None, :]).astype(jnp.bfloat16)
    keys_rot = with_rope(latent, cosine_table, sine_table).astype(jnp.bfloat16)
    blocks = ancestors.shape[0]
    width = LAT + ROPE
    key_blocks = keys_rot.reshape(blocks, BS, width)
    query_blocks = query_rot.reshape(blocks, BS, HEADS, width)
    grad_blocks = grad_out.reshape(blocks, BS, HEADS, LAT)

    def one_block(totals, block):
        listed = ancestors[block]
        block_ids = jnp.concatenate([block[None], jnp.maximum(listed, 0)]).astype(jnp.int32)
        used = jnp.concatenate([jnp.ones((1,), bool), listed >= 0])
        keys = key_blocks[block_ids].reshape((ANC + 1) * BS, width).astype(jnp.float32)
        first_slot = jnp.arange(ANC + 1, dtype=jnp.int32)[:, None, None] == 0
        allowed = jnp.where(first_slot, closure[block][None] > 0.5, used[:, None, None])
        allowed = allowed.transpose(1, 0, 2).reshape(BS, (ANC + 1) * BS)
        queries = query_blocks[block].astype(jnp.float32)
        grads = grad_blocks[block].astype(jnp.float32)
        scores = jnp.einsum("qhd,kd->hqk", queries, keys) * score_scale
        scores = jnp.where(allowed[None], scores, -jnp.inf)
        largest = jnp.max(scores, axis=2, keepdims=True)
        expo = jnp.exp(scores - largest)
        weights = expo / jnp.sum(expo, axis=2, keepdims=True)
        weights_b = lax.optimization_barrier(weights.astype(jnp.bfloat16)).astype(jnp.float32)
        output = jnp.einsum("hqk,kd->qhd", weights_b, keys[:, :LAT])
        row_delta = jnp.sum(grads * output, axis=2)
        slope = jnp.einsum("qhd,kd->hqk", grads, keys[:, :LAT])
        dscore = score_scale * weights * (slope - row_delta.T[:, :, None])
        dscore = lax.optimization_barrier(dscore.astype(jnp.bfloat16)).astype(jnp.float32)
        grad_rot = jnp.einsum("hqk,kd->qhd", dscore, keys)
        grad_keys = jnp.einsum("hqk,qhd->kd", dscore, queries)
        grad_keys = grad_keys.at[:, :LAT].add(jnp.einsum("hqk,qhd->kd", weights_b, grads))
        totals = totals.at[block_ids].add(grad_keys.reshape(ANC + 1, BS, width))
        return totals, grad_rot

    start = jnp.zeros((blocks, BS, width), jnp.float32)
    totals, grad_rot = lax.scan(one_block, start, jnp.arange(blocks, dtype=jnp.int32))
    grad_rot = grad_rot.reshape(blocks * BS, HEADS, width)
    d_query = jnp.concatenate([grad_rot[..., :LAT], unrotate(grad_rot[..., LAT:], cosine_table[:, None, :], sine_table[:, None, :])], axis=-1).astype(jnp.bfloat16)
    totals = totals.reshape(blocks * BS, width)
    d_latent = jnp.concatenate([totals[:, :LAT], unrotate(totals[:, LAT:], cosine_table, sine_table)], axis=-1).astype(jnp.bfloat16)
    return d_query, d_latent
```

```python
import functools

import jax
import jax.numpy as jnp
import numpy as np
from jax import lax
from jax.experimental import pallas as pl
from jax.experimental.pallas import tpu as pltpu
from jax.sharding import PartitionSpec as P

LAT = 512
ROPE = 64
BS = 128
WIDTH = LAT + ROPE
HALF = BS // 2
SIDE = BS + HALF
REMOTE = 2 * SIDE
KEYS = BS + REMOTE
TILE = 256

score_scale = 192.0 ** (-0.5)
rope_base = 10000.0
exponent_scale = score_scale * float(np.log2(np.e))
MASKED = -1e30

BF = jnp.bfloat16
F32 = jnp.float32
NT = (((1,), (1,)), ((), ()))
NN = (((1,), (0,)), ((), ()))
TN = (((0,), (0,)), ((), ()))


def dot(a, b, dims):
    return lax.dot_general(a, b, dims, preferred_element_type=F32)


def vmem(shape, dtype):
    return pltpu.VMEM(shape, dtype)


def in_vmem(x):
    return pltpu.with_memory_space_constraint(x, pltpu.VMEM)


def whole():
    return pl.BlockSpec(memory_space=pltpu.VMEM)


def scalars():
    return pl.BlockSpec(memory_space=pltpu.SMEM)


def turn(values, table):
    half = ROPE // 2
    first, second, cosine, sine = values[:half], values[half:], table[:half], table[half:]
    return jnp.concatenate([first * cosine - second * sine, first * sine + second * cosine], axis=0)


def turn_back(values, table):
    half = ROPE // 2
    first, second, cosine, sine = values[:half], values[half:], table[:half], table[half:]
    return jnp.concatenate([first * cosine + second * sine, second * cosine - first * sine], axis=0)


def keys_kernel(core_ref, anc_ref, parents_ref, freq_ref, latent_ref, keys_ref, half_ref, table_ref, closure_ref):
    row = lax.broadcasted_iota(jnp.int32, (BS, BS), 0)
    col = lax.broadcasted_iota(jnp.int32, (BS, BS), 1)
    linked = (row == parents_ref[...]) | (row == col)
    closure = jnp.where(linked, 1.0, 0.0).astype(BF)
    for _ in range((BS - 1).bit_length()):
        reach = jnp.minimum(dot(closure, closure, NN), 1.0)
        closure = reach.astype(BF)
    closure_ref[...] = reach
    depth = jnp.sum(reach, axis=0, keepdims=True) - 1.0
    count = 0
    for k in range(anc_ref.shape[1]):
        count = count + (anc_ref[0, k] >= 0).astype(jnp.int32)
    angles = (depth + (BS * count).astype(F32)) * freq_ref[...]
    table = jnp.concatenate([jnp.cos(angles), jnp.sin(angles)], axis=0)
    table_ref[...] = table
    turned = turn(latent_ref[LAT:, :].astype(F32), table)
    for lo in range(0, LAT, BS):
        keys_ref[:, lo : lo + BS] = latent_ref[lo : lo + BS, :].T
    keys_ref[:, LAT:] = turned.T.astype(BF)
    half_ref[...] = keys_ref[pl.ds(pl.multiple_of(core_ref[0] * HALF, HALF), HALF), :]


def own_kernel(heads, query_ref, grad_ref, keys_ref, table_ref, closure_ref, cat_ref, sorted_ref, score_ref, slope_ref):
    rows = TILE // heads
    row = lax.broadcasted_iota(jnp.int32, (TILE, TILE), 0)
    col = lax.broadcasted_iota(jnp.int32, (TILE, TILE), 1)
    order = jnp.where(col == (row % rows) * heads + row // rows, 1.0, 0.0).astype(BF)

    def sort(t, carry):
        chunk = grad_ref[pl.ds(pl.multiple_of(t * TILE, TILE), TILE), :]
        chunk = dot(order, chunk, NN).astype(BF)
        for h in range(heads):
            at = pl.multiple_of(h * BS + t * rows, rows)
            sorted_ref[pl.ds(at, rows), :] = chunk[h * rows : (h + 1) * rows]
        return carry

    lax.fori_loop(0, BS // rows, sort, 0)
    table = table_ref[...]
    seen = jnp.concatenate([closure_ref[...]] * (TILE // BS), axis=1) > 0.5

    def step(t, carry):
        here = pl.ds(pl.multiple_of(t * TILE, TILE), TILE)
        for k in range(TILE // BS):
            lanes = pl.ds(pl.multiple_of(t * TILE + k * BS, BS), BS)
            at = pl.multiple_of((t * (TILE // BS) + k) * WIDTH, ROPE)
            cat_ref[:LAT, lanes] = query_ref[pl.ds(at, LAT), :]
            cat_ref[LAT:, lanes] = turn(query_ref[pl.ds(at + LAT, ROPE), :].astype(F32), table).astype(BF)
        score = dot(keys_ref[...], cat_ref[:, here], NN)
        score_ref[:, here] = jnp.where(seen, score * exponent_scale, MASKED)
        slope_ref[:, here] = dot(keys_ref[:, :LAT], sorted_ref[here, :], NT)
        return carry

    lax.fori_loop(0, heads * BS // TILE, step, 0)


def key_grads(rows, weight_ref, dscore_ref, cat_ref, sorted_ref):
    turned = dot(dscore_ref[rows, :], cat_ref[...], NT) * score_scale
    plain = dot(weight_ref[rows, :], sorted_ref[...], NN)
    return turned[:, :LAT] + plain, turned[:, LAT:]


def main_kernel(bias_ref, cat_ref, sorted_ref, mine_ref, other_ref, score_ref, slope_ref,
                weight_ref, dscore_ref, gmine_ref, gother_ref):
    total = cat_ref.shape[1]
    bounds = ((0, BS), (BS, SIDE))

    def step(t, carry):
        here = pl.ds(pl.multiple_of(t * TILE, TILE), TILE)
        query = cat_ref[:, here]
        grad = sorted_ref[here, :]
        scores, slopes, biases = [score_ref[:, here]], [slope_ref[:, here]], [0.0]
        for side, ref in enumerate((mine_ref, other_ref)):
            score = dot(ref[...], query, NN) * exponent_scale
            slope = dot(ref[:, :LAT], grad, NT)
            for part, (lo, hi) in enumerate(bounds):
                scores.append(score[lo:hi])
                slopes.append(slope[lo:hi])
                biases.append(bias_ref[2 * side + part])
        largest = functools.reduce(
            jnp.maximum, [jnp.max(s, axis=0, keepdims=True) + b for s, b in zip(scores, biases)]
        )
        expos = [jnp.exp2(s - (largest - b)) for s, b in zip(scores, biases)]
        inverse = 1.0 / sum(jnp.sum(e, axis=0, keepdims=True) for e in expos)
        delta = sum(jnp.sum(e * s, axis=0, keepdims=True) for e, s in zip(expos, slopes)) * inverse
        at = 0
        for e, s in zip(expos, slopes):
            rows = pl.ds(at, e.shape[0])
            weight = e * inverse
            weight_ref[rows, here] = weight.astype(BF)
            dscore_ref[rows, here] = (weight * (s - delta)).astype(BF)
            at += e.shape[0]
        return carry

    lax.fori_loop(0, total // TILE, step, 0)
    for out, lo in ((gother_ref, BS + SIDE), (gmine_ref, BS)):
        lead, tail = key_grads(pl.ds(lo, SIDE), weight_ref, dscore_ref, cat_ref, sorted_ref)
        out[:, :LAT] = lead.astype(out.dtype)
        out[:, LAT:] = tail.astype(out.dtype)


def query_kernel(weight_ref, dscore_ref, cat_ref, sorted_ref, keys_ref, mine_ref, other_ref, table_ref,
                 dquery_ref, gown_ref, every_ref, turned_ref):
    t = pl.program_id(0)

    @pl.when(t == 0)
    def _():
        every_ref[:BS, :] = keys_ref[...]
        every_ref[BS : BS + SIDE, :] = mine_ref[...]
        every_ref[BS + SIDE :, :] = other_ref[...]
        for lo in range(0, KEYS, BS):
            turned_ref[:, lo : lo + BS] = every_ref[lo : lo + BS, :].T
        lead, tail = key_grads(pl.ds(0, BS), weight_ref, dscore_ref, cat_ref, sorted_ref)
        gown_ref[:, :LAT] = lead
        gown_ref[:, LAT:] = tail

    dscore = dscore_ref[:, pl.ds(pl.multiple_of(t * TILE, TILE), TILE)]
    grads = dot(turned_ref[...], dscore, NN) * score_scale
    for k in range(TILE // BS):
        part = grads[:, k * BS : (k + 1) * BS]
        dquery_ref[k, :LAT, :] = part[:LAT].astype(BF)
        dquery_ref[k, LAT:, :] = turn_back(part[LAT:], table_ref[...]).astype(BF)


def finish_kernel(core_ref, chip_ref, near_ref, far_ref, rest_ref, table_ref, out_ref, sum_ref):
    core = core_ref[0]
    sum_ref[...] = chip_ref[...].astype(F32)
    mine = pl.ds(pl.multiple_of(core * HALF, HALF), HALF)
    other = pl.ds(pl.multiple_of((1 - core) * HALF, HALF), HALF)
    sum_ref[mine, :] += far_ref[...].astype(F32)
    sum_ref[other, :] += rest_ref[BS:, :].astype(F32)
    sum_ref[...] += near_ref[...].astype(F32) + rest_ref[:BS, :].astype(F32)
    for lo in range(0, LAT, BS):
        out_ref[lo : lo + BS, :] = sum_ref[:, lo : lo + BS].T.astype(BF)
    out_ref[LAT:, :] = turn_back(sum_ref[:, LAT:].T, table_ref[...]).astype(BF)


def by_core(block, even, odd):
    tp, cp = lax.axis_size("tp"), lax.axis_size("cp")
    route = []
    for t in range(tp):
        step = odd if t % 2 else even
        for c in range(cp):
            if 0 <= c + step < cp or WRAP:
                route.append((t * cp + c, t * cp + (c + step) % cp))
    return lax.ppermute(block, ("tp", "cp"), route)


WRAP = True


def other_core(block):
    return lax.ppermute(block, "tp", [(t, t ^ 1) for t in range(lax.axis_size("tp"))])


def along_x(block, even, odd):
    tp = lax.axis_size("tp")
    route = [(t, (t + 2 * (odd if t % 2 else even)) % tp) for t in range(tp)]
    return lax.ppermute(block, "tp", route)


def halves(core, mine, other):
    return jnp.where(core == 0, jnp.concatenate([mine, other]), jnp.concatenate([other, mine]))


def on_device(query, latent, grad_out, ancestors, parents):
    rows, heads, _ = query.shape
    total = rows * heads
    core = lax.axis_index("tp") % 2
    here = lax.axis_index("cp")
    core_index = core.reshape(1).astype(jnp.int32)
    q = in_vmem(query.transpose(1, 2, 0).reshape(heads * WIDTH, rows))
    g = in_vmem(grad_out.reshape(total, LAT))
    half = ROPE // 2
    lane_freq = rope_base ** (-2.0 * np.arange(half, dtype=np.float64) / ROPE)
    freq = jnp.asarray(np.tile(lane_freq[:, None], (1, BS)), dtype=F32)
    params = pltpu.CompilerParams(vmem_limit_bytes=40 * 2**20)

    keys, keys_half, table, closure = pl.pallas_call(
        keys_kernel,
        in_specs=[scalars(), scalars(), whole(), whole(), whole()],
        out_specs=[whole()] * 4,
        out_shape=[vmem((BS, WIDTH), BF), vmem((HALF, WIDTH), BF), vmem((ROPE, BS), F32), vmem((BS, BS), F32)],
        name="keys",
    )(core_index, ancestors, parents.reshape(1, BS), freq, latent.T)

    fetched = by_core(keys, 1, 2)
    fetched_half = by_core(keys_half, 3, 3)

    cat, ordered, score_own, slope_own = pl.pallas_call(
        functools.partial(own_kernel, heads),
        in_specs=[whole()] * 5,
        out_specs=[whole()] * 4,
        out_shape=[vmem((WIDTH, total), BF), vmem((total, LAT), BF), vmem((BS, total), F32), vmem((BS, total), F32)],
        cost_estimate=pl.CostEstimate(flops=2 * total * BS * 1800, bytes_accessed=4 * total * WIDTH, transcendentals=0),
        compiler_params=params,
        name="own",
    )(q, g, keys, table, closure)

    mine = jnp.concatenate([fetched, fetched_half])
    other = other_core(mine)

    offsets = jnp.where(core == 0, jnp.array([1, 3, 2, 3]), jnp.array([2, 3, 1, 3]))
    ids = here - offsets
    listed = jnp.any((ids[:, None] == ancestors[0][None, :]) & (ids[:, None] >= 0), axis=1)
    bias = jnp.where(listed, 0.0, MASKED).astype(F32)

    weight, dscore, gmine, gother = pl.pallas_call(
        main_kernel,
        in_specs=[scalars()] + [whole()] * 6,
        out_specs=[whole()] * 4,
        out_shape=[vmem((KEYS, total), BF), vmem((KEYS, total), BF), vmem((SIDE, WIDTH), F32), vmem((SIDE, WIDTH), BF)],
        cost_estimate=pl.CostEstimate(flops=2 * total * REMOTE * 2560, bytes_accessed=8 * total * WIDTH, transcendentals=total * KEYS),
        compiler_params=params,
        name="main",
    )(bias, cat, ordered, mine, other, score_own, slope_own)

    gmine = (gmine + other_core(gother).astype(F32)).astype(BF)
    back = by_core(gmine[:BS], -1, -2)
    back_half = by_core(gmine[BS:], -3, -3)

    dquery, gown = pl.pallas_call(
        query_kernel,
        grid=(total // TILE,),
        in_specs=[whole()] * 8,
        out_specs=[pl.BlockSpec((TILE // BS, WIDTH, BS), lambda t: (t, 0, 0)), whole()],
        out_shape=[jax.ShapeDtypeStruct((heads, WIDTH, rows), BF), vmem((BS, WIDTH), F32)],
        scratch_shapes=[pltpu.VMEM((KEYS, WIDTH), BF), pltpu.VMEM((WIDTH, KEYS), BF)],
        cost_estimate=pl.CostEstimate(flops=2 * total * KEYS * 900, bytes_accessed=4 * total * WIDTH, transcendentals=0),
        compiler_params=params,
        name="dquery",
    )(weight, dscore, cat, ordered, keys, mine, other, table)

    back_half = back_half.astype(F32)
    nothing = jnp.zeros_like(back_half)
    device_sum = (gown + back.astype(F32) + halves(core, back_half, nothing)).astype(BF)
    chip_sum = (device_sum.astype(F32) + other_core(device_sum).astype(F32)).astype(BF)
    near = along_x(chip_sum, 1, -1)
    far = along_x(lax.dynamic_slice_in_dim(chip_sum, core * HALF, HALF), 2, 2)
    rest = other_core(jnp.concatenate([near, far]))
    d_latent = pl.pallas_call(
        finish_kernel,
        in_specs=[scalars()] + [whole()] * 5,
        out_specs=whole(),
        out_shape=jax.ShapeDtypeStruct((WIDTH, BS), BF),
        scratch_shapes=[pltpu.VMEM((BS, WIDTH), F32)],
        name="finish",
    )(core_index, chip_sum, near, far, rest, table)
    return (dquery.transpose(2, 0, 1), d_latent.T)


def solution(mesh):
    placed = (P("cp", "tp", None), P("cp", None), P("cp", "tp", None), P("cp", None), P("cp"))
    return jax.shard_map(
        on_device,
        mesh=mesh,
        in_specs=placed,
        out_specs=(P("cp", "tp", None), P("cp", None)),
        check_vma=False,
    )
```

```python
import functools

import jax
import jax.numpy as jnp
import numpy as np
from jax import lax
from jax.experimental import pallas as pl
from jax.experimental.pallas import tpu as pltpu
from jax.sharding import PartitionSpec as P

LAT = 512
ROPE = 64
BS = 128
WIDTH = LAT + ROPE
HALF = BS // 2
SIDE = BS + HALF
REMOTE = 2 * SIDE
KEYS = BS + REMOTE
TILE = 256
STEP = 1024

score_scale = 192.0 ** (-0.5)
rope_base = 10000.0
exponent_scale = score_scale * float(np.log2(np.e))
MASKED = -1e30

BF = jnp.bfloat16
F32 = jnp.float32
NT = (((1,), (1,)), ((), ()))
NN = (((1,), (0,)), ((), ()))
TN = (((0,), (0,)), ((), ()))


def dot(a, b, dims):
    return lax.dot_general(a, b, dims, preferred_element_type=F32)


def vmem(shape, dtype):
    return pltpu.VMEM(shape, dtype)


def in_vmem(x):
    return pltpu.with_memory_space_constraint(x, pltpu.VMEM)


def in_hbm(x):
    return pltpu.with_memory_space_constraint(x, pltpu.HBM)


def whole():
    return pl.BlockSpec(memory_space=pltpu.VMEM)


def scalars():
    return pl.BlockSpec(memory_space=pltpu.SMEM)


def turn(values, table):
    half = ROPE // 2
    first, second, cosine, sine = values[:half], values[half:], table[:half], table[half:]
    return jnp.concatenate([first * cosine - second * sine, first * sine + second * cosine], axis=0)


def turn_back(values, table):
    half = ROPE // 2
    first, second, cosine, sine = values[:half], values[half:], table[:half], table[half:]
    return jnp.concatenate([first * cosine + second * sine, second * cosine - first * sine], axis=0)


def this_core():
    return lax.rem(lax.axis_index("tp"), 2)


def keys_kernel(anc_ref, parents_ref, freq_ref, latent_ref, keys_ref, half_ref, table_ref, closure_ref):
    row = lax.broadcasted_iota(jnp.int32, (BS, BS), 0)
    col = lax.broadcasted_iota(jnp.int32, (BS, BS), 1)
    linked = (row == parents_ref[...]) | (row == col)
    closure = jnp.where(linked, 1.0, 0.0).astype(BF)
    for _ in range((BS - 1).bit_length()):
        reach = jnp.minimum(dot(closure, closure, NN), 1.0)
        closure = reach.astype(BF)
    closure_ref[...] = reach
    depth = jnp.sum(reach, axis=0, keepdims=True) - 1.0
    count = 0
    for k in range(anc_ref.shape[1]):
        count = count + (anc_ref[0, k] >= 0).astype(jnp.int32)
    angles = (depth + (BS * count).astype(F32)) * freq_ref[...]
    table = jnp.concatenate([jnp.cos(angles), jnp.sin(angles)], axis=0)
    table_ref[...] = table
    for lo in range(0, LAT, BS):
        keys_ref[:, lo : lo + BS] = latent_ref[lo : lo + BS, :].T
    turned = turn(latent_ref[LAT:, :].astype(F32), table)
    keys_ref[:, LAT:] = turned.T.astype(BF)
    half_ref[...] = keys_ref[own_half(), :]


def own_kernel(heads, query_hbm, grad_hbm, keys_ref, table_ref, closure_ref, cat_ref, sorted_ref, score_ref, slope_ref,
               query_ref, grad_ref, sems):
    pieces = heads * BS // TILE
    pair = TILE // BS * WIDTH
    grad_copies, query_copies = [], []
    for t in range(pieces):
        at = pl.ds(t * TILE, TILE)
        grad_copies.append(pltpu.make_async_copy(grad_hbm.at[at], grad_ref.at[at], sems.at[t]))
    for t in range(pieces):
        at = pl.ds(t * pair, pair)
        query_copies.append(pltpu.make_async_copy(query_hbm.at[at], query_ref.at[at], sems.at[pieces + t]))
    for copy in grad_copies + query_copies:
        copy.start()
    rows = TILE // heads
    row = lax.broadcasted_iota(jnp.int32, (TILE, TILE), 0)
    col = lax.broadcasted_iota(jnp.int32, (TILE, TILE), 1)
    order = jnp.where(col == (row % rows) * heads + row // rows, 1.0, 0.0).astype(BF)
    for t in range(pieces):
        grad_copies[t].wait()
        chunk = dot(order, grad_ref[t * TILE : (t + 1) * TILE, :], NN).astype(BF)
        for h in range(heads):
            sorted_ref[pl.ds(h * BS + t * rows, rows), :] = chunk[h * rows : (h + 1) * rows]
    table = table_ref[...]
    seen = jnp.concatenate([closure_ref[...]] * (TILE // BS), axis=1) > 0.5
    for t in range(pieces):
        query_copies[t].wait()
        here = pl.ds(t * TILE, TILE)
        for k in range(TILE // BS):
            lanes = pl.ds(t * TILE + k * BS, BS)
            at = t * pair + k * WIDTH
            cat_ref[:LAT, lanes] = query_ref[pl.ds(at, LAT), :]
            cat_ref[LAT:, lanes] = turn(query_ref[pl.ds(at + LAT, ROPE), :].astype(F32), table).astype(BF)
        score = dot(keys_ref[...], cat_ref[:, here], NN)
        score_ref[:, here] = jnp.where(seen, score * exponent_scale, MASKED)
        slope_ref[:, here] = dot(keys_ref[:, :LAT], sorted_ref[here, :], NT)


def key_grads(rows, weight_ref, dscore_ref, cat_ref, sorted_ref):
    turned = dot(dscore_ref[rows, :], cat_ref[...], NT) * score_scale
    plain = dot(weight_ref[rows, :], sorted_ref[...], NN)
    return turned[:, :LAT] + plain, turned[:, LAT:]


def mine_kernel(cat_ref, sorted_ref, mine_ref, score_ref, slope_ref):
    for lo in range(0, cat_ref.shape[1], TILE):
        here = pl.ds(lo, TILE)
        score_ref[:, here] = dot(mine_ref[...], cat_ref[:, here], NN) * exponent_scale
        slope_ref[:, here] = dot(mine_ref[:, :LAT], sorted_ref[here, :], NT)


def main_kernel(anc_ref, cat_ref, sorted_ref, other_ref, own_score, own_slope, mine_score, mine_slope,
                weight_ref, dscore_ref, gother_ref, score_ref, slope_ref):
    tiles = cat_ref.shape[1] // TILE
    core, block = this_core(), lax.axis_index("cp")

    def bias(offset):
        wanted = block - offset
        listed = jnp.int32(0)
        for k in range(anc_ref.shape[1]):
            listed = jnp.where(anc_ref[0, k] == wanted, 1, listed)
        return jnp.where((wanted >= 0) & (listed > 0), 0.0, MASKED).astype(F32)

    whole_mine, whole_other, part = bias(1 + core), bias(2 - core), bias(3)

    def products(t):
        here = pl.ds(t * TILE, TILE)
        score_ref[t % 2] = dot(other_ref[...], cat_ref[:, here], NN) * exponent_scale
        slope_ref[t % 2] = dot(other_ref[:, :LAT], sorted_ref[here, :], NT)

    def softmax(t):
        here = pl.ds(t * TILE, TILE)
        places = (
            (own_score[:, here], own_slope[:, here], 0.0),
            (mine_score[:BS, here], mine_slope[:BS, here], whole_mine),
            (mine_score[BS:, here], mine_slope[BS:, here], part),
            (score_ref[t % 2, :BS], slope_ref[t % 2, :BS], whole_other),
            (score_ref[t % 2, BS:], slope_ref[t % 2, BS:], part),
        )
        largest = functools.reduce(jnp.maximum, [jnp.max(s, axis=0, keepdims=True) + b for s, _, b in places])
        expos = [jnp.exp2(s - (largest - b)) for s, _, b in places]
        inverse = 1.0 / sum(jnp.sum(e, axis=0, keepdims=True) for e in expos)
        delta = sum(jnp.sum(e * l, axis=0, keepdims=True) for e, (_, l, _) in zip(expos, places)) * inverse
        at = 0
        for e, (_, l, _) in zip(expos, places):
            rows = pl.ds(at, e.shape[0])
            weight = e * inverse
            weight_ref[rows, here] = weight.astype(BF)
            dscore_ref[rows, here] = (weight * (l - delta)).astype(BF)
            at += e.shape[0]

    products(0)
    for t in range(tiles):
        if t + 1 < tiles:
            products(t + 1)
        softmax(t)
    lead, tail = key_grads(pl.ds(BS + SIDE, SIDE), weight_ref, dscore_ref, cat_ref, sorted_ref)
    gother_ref[:, :LAT] = lead.astype(BF)
    gother_ref[:, LAT:] = tail.astype(BF)


def grads_kernel(weight_ref, dscore_ref, cat_ref, sorted_ref, gmine_ref):
    lead, tail = key_grads(pl.ds(BS, SIDE), weight_ref, dscore_ref, cat_ref, sorted_ref)
    gmine_ref[:, :LAT] = lead
    gmine_ref[:, LAT:] = tail


def query_kernel(weight_ref, dscore_ref, cat_ref, sorted_ref, keys_ref, mine_ref, other_ref, table_ref,
                 dquery_ref, gown_ref, every_ref, turned_ref):
    t = pl.program_id(0)

    @pl.when(t == 0)
    def _():
        every_ref[:BS, :] = keys_ref[...]
        every_ref[BS : BS + SIDE, :] = mine_ref[...]
        every_ref[BS + SIDE :, :] = other_ref[...]
        for lo in range(0, KEYS, BS):
            turned_ref[:, lo : lo + BS] = every_ref[lo : lo + BS, :].T
        lead, tail = key_grads(pl.ds(0, BS), weight_ref, dscore_ref, cat_ref, sorted_ref)
        gown_ref[:, :LAT] = lead
        gown_ref[:, LAT:] = tail

    dscore = dscore_ref[:, pl.ds(pl.multiple_of(t * STEP, STEP), STEP)]
    grads = dot(turned_ref[...], dscore, NN) * score_scale
    for k in range(STEP // BS):
        part = grads[:, k * BS : (k + 1) * BS]
        dquery_ref[k, :LAT, :] = part[:LAT].astype(BF)
        dquery_ref[k, LAT:, :] = turn_back(part[LAT:], table_ref[...]).astype(BF)


def own_half():
    return pl.ds(pl.multiple_of(this_core() * HALF, HALF), HALF)


def other_half():
    return pl.ds(pl.multiple_of((1 - this_core()) * HALF, HALF), HALF)


def device_kernel(gown_ref, back_ref, half_ref, out_ref, sum_ref):
    sum_ref[...] = gown_ref[...] + back_ref[...].astype(F32)
    sum_ref[own_half(), :] += half_ref[...].astype(F32)
    out_ref[...] = sum_ref[...].astype(BF)


def chip_kernel(device_ref, other_ref, chip_ref, half_ref):
    chip_ref[...] = (device_ref[...].astype(F32) + other_ref[...].astype(F32)).astype(BF)
    half_ref[...] = chip_ref[own_half(), :]


def finish_kernel(chip_ref, near_ref, far_ref, rest_ref, table_ref, out_ref, sum_ref):
    sum_ref[...] = chip_ref[...].astype(F32)
    sum_ref[own_half(), :] += far_ref[...].astype(F32)
    sum_ref[other_half(), :] += rest_ref[BS:, :].astype(F32)
    sum_ref[...] += near_ref[...].astype(F32) + rest_ref[:BS, :].astype(F32)
    for lo in range(0, LAT, BS):
        out_ref[lo : lo + BS, :] = sum_ref[:, lo : lo + BS].T.astype(BF)
    out_ref[LAT:, :] = turn_back(sum_ref[:, LAT:].T, table_ref[...]).astype(BF)


def by_core(block, even, odd):
    tp, cp = lax.axis_size("tp"), lax.axis_size("cp")
    route = []
    for t in range(tp):
        step = odd if t % 2 else even
        for c in range(cp):
            if 0 <= c + step < cp or WRAP:
                route.append((t * cp + c, t * cp + (c + step) % cp))
    return lax.ppermute(block, ("tp", "cp"), route)


WRAP = True


def other_core(block):
    return lax.ppermute(block, "tp", [(t, t ^ 1) for t in range(lax.axis_size("tp"))])


def along_x(block, even, odd):
    tp = lax.axis_size("tp")
    route = [(t, (t + 2 * (odd if t % 2 else even)) % tp) for t in range(tp)]
    return lax.ppermute(block, "tp", route)


def on_device(query, latent, grad_out, ancestors, parents):
    rows, heads, _ = query.shape
    total = rows * heads
    half = ROPE // 2
    lane_freq = rope_base ** (-2.0 * np.arange(half, dtype=np.float64) / ROPE)
    freq = jnp.asarray(np.tile(lane_freq[:, None], (1, BS)), dtype=F32)
    params = pltpu.CompilerParams(vmem_limit_bytes=16 * 2**20)
    outside = pl.BlockSpec(memory_space=pltpu.HBM)

    def call(kernel, name, ins, outs, flops=0, **more):
        return pl.pallas_call(
            kernel,
            in_specs=ins,
            out_specs=[whole()] * len(outs),
            out_shape=[vmem(*o) for o in outs],
            cost_estimate=pl.CostEstimate(flops=flops, bytes_accessed=4 * total * WIDTH, transcendentals=0),
            compiler_params=params,
            name=name,
            **more,
        )

    keys, keys_half, table, closure = call(
        keys_kernel,
        "keys",
        [scalars(), whole(), whole(), whole()],
        [((BS, WIDTH), BF), ((HALF, WIDTH), BF), ((ROPE, BS), F32), ((BS, BS), F32)],
    )(*map(in_hbm, (ancestors, parents.reshape(1, BS), freq, latent.T)))

    fetched = by_core(keys, 1, 2)
    fetched_half = by_core(keys_half, 3, 3)

    cat, ordered, own_score, own_slope = call(
        functools.partial(own_kernel, heads),
        "own",
        [outside] * 2 + [whole()] * 3,
        [((WIDTH, total), BF), ((total, LAT), BF), ((BS, total), F32), ((BS, total), F32)],
        flops=2 * total * BS * 1800,
        scratch_shapes=[
            pltpu.VMEM((heads * WIDTH, rows), BF),
            pltpu.VMEM((total, LAT), BF),
            pltpu.SemaphoreType.DMA((2 * total // TILE,)),
        ],
    )(in_hbm(query.transpose(1, 2, 0).reshape(heads * WIDTH, rows)), in_hbm(grad_out.reshape(total, LAT)),
      keys, table, closure)

    mine, cat = lax.optimization_barrier((jnp.concatenate([fetched, fetched_half]), cat))
    other = other_core(mine)
    mine_score, mine_slope = call(
        mine_kernel, "mine", [whole()] * 3, [((SIDE, total), F32), ((SIDE, total), F32)], flops=2 * total * SIDE * 1280
    )(cat, ordered, mine)

    weight, dscore, gother = call(
        main_kernel,
        "main",
        [scalars()] + [whole()] * 7,
        [((KEYS, total), BF), ((KEYS, total), BF), ((SIDE, WIDTH), BF)],
        flops=2 * total * SIDE * 2560,
        scratch_shapes=[pltpu.VMEM((2, SIDE, TILE), F32), pltpu.VMEM((2, SIDE, TILE), F32)],
    )(in_hbm(ancestors), cat, ordered, other, own_score, own_slope, mine_score, mine_slope)

    gother = other_core(gother)
    (gmine,) = call(
        grads_kernel, "grads", [whole()] * 4, [((SIDE, WIDTH), F32)], flops=2 * total * SIDE * 1280
    )(weight, dscore, cat, ordered)
    gmine = (gmine + gother.astype(F32)).astype(BF)
    back = by_core(gmine[:BS], -1, -2)
    back_half = by_core(gmine[BS:], -3, -3)

    dquery, gown = pl.pallas_call(
        query_kernel,
        grid=(total // STEP,),
        in_specs=[whole()] * 8,
        out_specs=[pl.BlockSpec((STEP // BS, WIDTH, BS), lambda t: (t, 0, 0)), whole()],
        out_shape=[jax.ShapeDtypeStruct((heads, WIDTH, rows), BF), vmem((BS, WIDTH), F32)],
        scratch_shapes=[pltpu.VMEM((KEYS, WIDTH), BF), pltpu.VMEM((WIDTH, KEYS), BF)],
        cost_estimate=pl.CostEstimate(flops=2 * total * KEYS * 900, bytes_accessed=4 * total * WIDTH, transcendentals=0),
        compiler_params=params,
        name="dquery",
    )(weight, dscore, cat, ordered, keys, mine, other, table)

    (device_sum,) = call(
        device_kernel,
        "device",
        [whole()] * 3,
        [((BS, WIDTH), BF)],
        scratch_shapes=[pltpu.VMEM((BS, WIDTH), F32)],
    )(gown, back, back_half)
    chip_sum, chip_half = call(
        chip_kernel, "chip", [whole()] * 2, [((BS, WIDTH), BF), ((HALF, WIDTH), BF)]
    )(device_sum, other_core(device_sum))
    near = along_x(chip_sum, 1, -1)
    far = along_x(chip_half, 2, 2)
    rest = other_core(jnp.concatenate([near, far]))
    d_latent = pl.pallas_call(
        finish_kernel,
        in_specs=[whole()] * 5,
        out_specs=whole(),
        out_shape=jax.ShapeDtypeStruct((WIDTH, BS), BF),
        scratch_shapes=[pltpu.VMEM((BS, WIDTH), F32)],
        compiler_params=params,
        name="finish",
    )(*map(in_vmem, (chip_sum, near, far, rest, table)))
    return (dquery.transpose(2, 0, 1), d_latent.T)


def solution(mesh):
    placed = (P("cp", "tp", None), P("cp", None), P("cp", "tp", None), P("cp", None), P("cp"))
    return jax.shard_map(
        on_device,
        mesh=mesh,
        in_specs=placed,
        out_specs=(P("cp", "tp", None), P("cp", None)),
        check_vma=False,
    )
```

```python
import functools

import jax
import jax.numpy as jnp
import numpy as np
from jax import lax
from jax.experimental import pallas as pl
from jax.experimental.pallas import tpu as pltpu
from jax.sharding import PartitionSpec as P

LAT = 512
ROPE = 64
BS = 128
WIDTH = LAT + ROPE
HALF = BS // 2
SIDE = BS + HALF
REMOTE = 2 * SIDE
KEYS = BS + REMOTE
TILE = 256
STEP = 1024

score_scale = 192.0 ** (-0.5)
rope_base = 10000.0
exponent_scale = score_scale * float(np.log2(np.e))
MASKED = -1e30

BF = jnp.bfloat16
F32 = jnp.float32
NT = (((1,), (1,)), ((), ()))
NN = (((1,), (0,)), ((), ()))
TN = (((0,), (0,)), ((), ()))


def dot(a, b, dims):
    return lax.dot_general(a, b, dims, preferred_element_type=F32)


def vmem(shape, dtype):
    return pltpu.VMEM(shape, dtype)


def in_vmem(x):
    return pltpu.with_memory_space_constraint(x, pltpu.VMEM)


def in_hbm(x):
    return pltpu.with_memory_space_constraint(x, pltpu.HBM)


def whole():
    return pl.BlockSpec(memory_space=pltpu.VMEM)


def scalars():
    return pl.BlockSpec(memory_space=pltpu.SMEM)


def turn(values, table):
    half = ROPE // 2
    first, second, cosine, sine = values[:half], values[half:], table[:half], table[half:]
    return jnp.concatenate([first * cosine - second * sine, first * sine + second * cosine], axis=0)


def turn_back(values, table):
    half = ROPE // 2
    first, second, cosine, sine = values[:half], values[half:], table[:half], table[half:]
    return jnp.concatenate([first * cosine + second * sine, second * cosine - first * sine], axis=0)


def heads_of(ref, first, count, rows=(0, WIDTH)):
    lo, hi = rows
    return jnp.concatenate([ref[h * WIDTH + lo : h * WIDTH + hi, :] for h in range(first, first + count)], axis=1)


def this_core():
    return lax.rem(lax.axis_index("tp"), 2)


def keys_kernel(anc_ref, parents_ref, freq_hbm, latent_hbm, grad_hbm,
                keys_ref, half_ref, table_ref, closure_ref, bias_ref, grad_ref, freq_ref, latent_ref, sems):
    first = grad_hbm.at[pl.ds(0, grad_ref.shape[0])]
    copies = [
        pltpu.make_async_copy(source, target, sems.at[k])
        for k, (source, target) in enumerate(((latent_hbm, latent_ref), (freq_hbm, freq_ref), (first, grad_ref)))
    ]
    for copy in copies:
        copy.start()
    row = lax.broadcasted_iota(jnp.int32, (BS, BS), 0)
    col = lax.broadcasted_iota(jnp.int32, (BS, BS), 1)
    linked = (row == parents_ref[...]) | (row == col)

    def sweep(closure):
        return jnp.minimum(dot(closure.astype(BF), closure.astype(BF), NN), 1.0)

    reach = jnp.where(linked, 1.0, 0.0)
    early = 4
    for _ in range(early):
        reach = sweep(reach)
    closure_ref[...] = reach

    @pl.when(jnp.max(jnp.sum(reach, axis=0, keepdims=True)) > 2.0**early)
    def _():
        deep = closure_ref[...]
        for _ in range((BS - 1).bit_length() - early):
            deep = sweep(deep)
        closure_ref[...] = deep

    depth = jnp.sum(closure_ref[...], axis=0, keepdims=True) - 1.0
    block, core = lax.axis_index("cp"), this_core()
    count = 0
    for k in range(anc_ref.shape[1]):
        count = count + (anc_ref[0, k] >= 0).astype(jnp.int32)

    def bias(offset):
        wanted = block - offset
        listed = jnp.int32(0)
        for k in range(anc_ref.shape[1]):
            listed = jnp.where(anc_ref[0, k] == wanted, 1, listed)
        return jnp.where((wanted >= 0) & (listed > 0), 0.0, MASKED).astype(F32)

    for k, offset in enumerate((1 + core, 3, 2 - core, 3)):
        bias_ref[k : k + 1, :] = jnp.full((1, TILE), bias(offset), F32)
    bias_ref[4:, :] = jnp.zeros((4, TILE), F32)
    copies[1].wait()
    angles = (depth + (BS * count).astype(F32)) * freq_ref[...]
    table = jnp.concatenate([jnp.cos(angles), jnp.sin(angles)], axis=0)
    table_ref[...] = table
    copies[0].wait()
    for lo in range(0, LAT, BS):
        keys_ref[:, lo : lo + BS] = latent_ref[lo : lo + BS, :].T
    turned = turn(latent_ref[LAT:, :].astype(F32), table)
    keys_ref[:, LAT:] = turned.T.astype(BF)
    half_ref[...] = keys_ref[own_half(), :]
    copies[2].wait()


def own_kernel(heads, query_hbm, grad_hbm, early_ref, keys_ref, table_ref, closure_ref,
               query_ref, sorted_ref, score_ref, slope_ref, late_ref, sems):
    per = TILE // BS
    pieces = heads // per
    pair = per * WIDTH
    late = late_ref.shape[0]
    grad_copy = pltpu.make_async_copy(grad_hbm.at[pl.ds(late, late)], late_ref, sems.at[pieces])
    grad_copy.start()
    copies = []
    for t in range(pieces):
        at = pl.ds(t * pair, pair)
        copies.append(pltpu.make_async_copy(query_hbm.at[at], query_ref.at[at], sems.at[t]))
    for copy in copies:
        copy.start()
    rows = TILE // heads
    row = lax.broadcasted_iota(jnp.int32, (TILE, TILE), 0)
    col = lax.broadcasted_iota(jnp.int32, (TILE, TILE), 1)
    order = jnp.where(col == (row % rows) * heads + row // rows, 1.0, 0.0).astype(BF)
    table = table_ref[...]
    seen = jnp.concatenate([closure_ref[...]] * per, axis=1) > 0.5
    for t in range(pieces):
        if t == pieces // 2:
            grad_copy.wait()
        source, at = (early_ref, t * TILE) if t < pieces // 2 else (late_ref, t * TILE - late)
        chunk = dot(order, source[at : at + TILE, :], NN).astype(BF)
        for h in range(heads):
            sorted_ref[pl.ds(h * BS + t * rows, rows), :] = chunk[h * rows : (h + 1) * rows]
    for copy in copies:
        copy.wait()
    for h in range(heads):
        tail = pl.ds(h * WIDTH + LAT, ROPE)
        query_ref[tail, :] = turn(query_ref[tail, :].astype(F32), table).astype(BF)
    for t in range(pieces):
        here = pl.ds(t * TILE, TILE)
        score = dot(keys_ref[...], heads_of(query_ref, per * t, per), NN)
        score_ref[:, here] = jnp.where(seen, score * exponent_scale, MASKED)
        slope_ref[:, here] = dot(keys_ref[:, :LAT], sorted_ref[here, :], NT)


def key_grads(rows, weight_ref, dscore_ref, query_ref, sorted_ref):
    heads = query_ref.shape[0] // WIDTH
    turned = dot(dscore_ref[rows, :], heads_of(query_ref, 0, heads), NT) * score_scale
    plain = dot(weight_ref[rows, :], sorted_ref[...], NN)
    return turned[:, :LAT] + plain, turned[:, LAT:]


def mine_kernel(query_ref, sorted_ref, mine_ref, score_ref, slope_ref):
    per = TILE // BS
    for t in range(sorted_ref.shape[0] // TILE):
        here = pl.ds(t * TILE, TILE)
        score_ref[:, here] = dot(mine_ref[...], heads_of(query_ref, per * t, per), NN) * exponent_scale
        slope_ref[:, here] = dot(mine_ref[:, :LAT], sorted_ref[here, :], NT)


def main_kernel(bias_ref, query_ref, sorted_ref, other_ref, own_score, own_slope, mine_score, mine_slope,
                weight_ref, dscore_ref, gother_ref, score_ref, slope_ref):
    tiles = sorted_ref.shape[0] // TILE
    per = TILE // BS
    whole_mine, part, whole_other, _ = (bias_ref[k : k + 1, :] for k in range(4))

    def products(t):
        here = pl.ds(t * TILE, TILE)
        score_ref[t % 2] = dot(other_ref[...], heads_of(query_ref, per * t, per), NN) * exponent_scale
        slope_ref[t % 2] = dot(other_ref[:, :LAT], sorted_ref[here, :], NT)

    def softmax(t):
        here = pl.ds(t * TILE, TILE)
        places = (
            (own_score[:, here], own_slope[:, here], 0.0),
            (mine_score[:BS, here], mine_slope[:BS, here], whole_mine),
            (mine_score[BS:, here], mine_slope[BS:, here], part),
            (score_ref[t % 2, :BS], slope_ref[t % 2, :BS], whole_other),
            (score_ref[t % 2, BS:], slope_ref[t % 2, BS:], part),
        )
        largest = functools.reduce(jnp.maximum, [jnp.max(s, axis=0, keepdims=True) + b for s, _, b in places])
        expos = [jnp.exp2(s - (largest - b)) for s, _, b in places]
        inverse = 1.0 / sum(jnp.sum(e, axis=0, keepdims=True) for e in expos)
        delta = sum(jnp.sum(e * l, axis=0, keepdims=True) for e, (_, l, _) in zip(expos, places)) * inverse
        at = 0
        for e, (_, l, _) in zip(expos, places):
            rows = pl.ds(at, e.shape[0])
            weight = e * inverse
            weight_ref[rows, here] = weight.astype(BF)
            dscore_ref[rows, here] = (weight * (l - delta)).astype(BF)
            at += e.shape[0]

    products(0)
    for t in range(tiles):
        if t + 1 < tiles:
            products(t + 1)
        softmax(t)
    lead, tail = key_grads(pl.ds(BS + SIDE, SIDE), weight_ref, dscore_ref, query_ref, sorted_ref)
    gother_ref[:, :LAT] = lead.astype(BF)
    gother_ref[:, LAT:] = tail.astype(BF)


def grads_kernel(rows, weight_ref, dscore_ref, query_ref, sorted_ref, out_ref):
    lead, tail = key_grads(rows, weight_ref, dscore_ref, query_ref, sorted_ref)
    out_ref[:, :LAT] = lead
    out_ref[:, LAT:] = tail


def query_kernel(dscore_ref, keys_ref, mine_ref, other_ref, table_ref, dquery_ref, every_ref, turned_ref):
    t = pl.program_id(0)

    @pl.when(t == 0)
    def _():
        every_ref[:BS, :] = keys_ref[...]
        every_ref[BS : BS + SIDE, :] = mine_ref[...]
        every_ref[BS + SIDE :, :] = other_ref[...]
        for lo in range(0, KEYS, BS):
            turned_ref[:, lo : lo + BS] = every_ref[lo : lo + BS, :].T

    dscore = dscore_ref[:, pl.ds(pl.multiple_of(t * STEP, STEP), STEP)]
    grads = dot(turned_ref[...], dscore, NN) * score_scale
    for k in range(STEP // BS):
        part = grads[:, k * BS : (k + 1) * BS]
        dquery_ref[k, :LAT, :] = part[:LAT].astype(BF)
        dquery_ref[k, LAT:, :] = turn_back(part[LAT:], table_ref[...]).astype(BF)


def own_half():
    return pl.ds(pl.multiple_of(this_core() * HALF, HALF), HALF)


def other_half():
    return pl.ds(pl.multiple_of((1 - this_core()) * HALF, HALF), HALF)


def device_kernel(gown_ref, back_ref, half_ref, out_ref, sum_ref):
    sum_ref[...] = gown_ref[...] + back_ref[...].astype(F32)
    sum_ref[own_half(), :] += half_ref[...].astype(F32)
    out_ref[...] = sum_ref[...].astype(BF)


def chip_kernel(device_ref, other_ref, chip_ref, half_ref):
    chip_ref[...] = (device_ref[...].astype(F32) + other_ref[...].astype(F32)).astype(BF)
    half_ref[...] = chip_ref[own_half(), :]


def finish_kernel(chip_ref, near_ref, far_ref, rest_ref, table_ref, out_ref, sum_ref):
    sum_ref[...] = chip_ref[...].astype(F32)
    sum_ref[own_half(), :] += far_ref[...].astype(F32)
    sum_ref[other_half(), :] += rest_ref[BS:, :].astype(F32)
    sum_ref[...] += near_ref[...].astype(F32) + rest_ref[:BS, :].astype(F32)
    for lo in range(0, LAT, BS):
        out_ref[lo : lo + BS, :] = sum_ref[:, lo : lo + BS].T.astype(BF)
    out_ref[LAT:, :] = turn_back(sum_ref[:, LAT:].T, table_ref[...]).astype(BF)


def by_core(block, even, odd):
    tp, cp = lax.axis_size("tp"), lax.axis_size("cp")
    route = []
    for t in range(tp):
        step = odd if t % 2 else even
        for c in range(cp):
            if 0 <= c + step < cp or WRAP:
                route.append((t * cp + c, t * cp + (c + step) % cp))
    return lax.ppermute(block, ("tp", "cp"), route)


WRAP = True


def other_core(block):
    return lax.ppermute(block, "tp", [(t, t ^ 1) for t in range(lax.axis_size("tp"))])


def along_x(block, even, odd):
    route = [(t, t ^ (2 * (odd if t % 2 else even))) for t in range(lax.axis_size("tp"))]
    return lax.ppermute(block, "tp", route)


def on_device(query, latent, grad_out, ancestors, parents):
    rows, heads, _ = query.shape
    total = rows * heads
    half = ROPE // 2
    lane_freq = rope_base ** (-2.0 * np.arange(half, dtype=np.float64) / ROPE)
    freq = jnp.asarray(np.tile(lane_freq[:, None], (1, BS)), dtype=F32)
    params = pltpu.CompilerParams(vmem_limit_bytes=16 * 2**20)
    outside = pl.BlockSpec(memory_space=pltpu.HBM)

    def call(kernel, name, ins, outs, flops=0, **more):
        return pl.pallas_call(
            kernel,
            in_specs=ins,
            out_specs=[whole()] * len(outs),
            out_shape=[vmem(*o) for o in outs],
            cost_estimate=pl.CostEstimate(flops=flops, bytes_accessed=4 * total * WIDTH, transcendentals=0),
            compiler_params=params,
            name=name,
            **more,
        )

    keys, keys_half, table, closure, bias, early = call(
        keys_kernel,
        "keys",
        [scalars(), whole(), outside, outside, outside],
        [((BS, WIDTH), BF), ((HALF, WIDTH), BF), ((ROPE, BS), F32), ((BS, BS), F32), ((8, TILE), F32), ((total // 2, LAT), BF)],
        scratch_shapes=[pltpu.VMEM((half, BS), F32), pltpu.VMEM((WIDTH, BS), BF), pltpu.SemaphoreType.DMA((3,))],
    )(*map(in_hbm, (ancestors, parents.reshape(1, BS), freq, latent.T, grad_out.reshape(total, LAT))))

    fetched = by_core(keys, 1, 2)
    fetched_half = by_core(keys_half, 3, 3)

    q, g, own_score, own_slope = call(
        functools.partial(own_kernel, heads),
        "own",
        [outside] * 2 + [whole()] * 4,
        [((heads * WIDTH, rows), BF), ((total, LAT), BF), ((BS, total), F32), ((BS, total), F32)],
        flops=2 * total * BS * 1800,
        scratch_shapes=[pltpu.VMEM((total // 2, LAT), BF), pltpu.SemaphoreType.DMA((total // TILE + 1,))],
    )(in_hbm(query.transpose(1, 2, 0).reshape(heads * WIDTH, rows)), in_hbm(grad_out.reshape(total, LAT)),
      early, keys, table, closure)

    mine, q = lax.optimization_barrier((jnp.concatenate([fetched, fetched_half]), q))
    other = other_core(mine)
    mine_score, mine_slope = call(
        mine_kernel, "mine", [whole()] * 3, [((SIDE, total), F32), ((SIDE, total), F32)], flops=2 * total * SIDE * 1280
    )(q, g, mine)

    weight, dscore, gother = call(
        main_kernel,
        "main",
        [whole()] * 8,
        [((KEYS, total), BF), ((KEYS, total), BF), ((SIDE, WIDTH), BF)],
        flops=2 * total * SIDE * 2560,
        scratch_shapes=[pltpu.VMEM((2, SIDE, TILE), F32), pltpu.VMEM((2, SIDE, TILE), F32)],
    )(bias, q, g, other, own_score, own_slope, mine_score, mine_slope)

    gother = other_core(gother)
    (gmine,) = call(
        functools.partial(grads_kernel, slice(BS, BS + SIDE)),
        "grads",
        [whole()] * 4,
        [((SIDE, WIDTH), F32)],
        flops=2 * total * SIDE * 1280,
    )(weight, dscore, q, g)
    gmine = (gmine + gother.astype(F32)).astype(BF)
    back = by_core(gmine[:BS], -1, -2)
    back_half = by_core(gmine[BS:], -3, -3)

    (gown,) = call(
        functools.partial(grads_kernel, slice(0, BS)),
        "gown",
        [whole()] * 4,
        [((BS, WIDTH), F32)],
        flops=2 * total * BS * 1280,
    )(weight, dscore, q, g)
    (device_sum,) = call(
        device_kernel,
        "device",
        [whole()] * 3,
        [((BS, WIDTH), BF)],
        scratch_shapes=[pltpu.VMEM((BS, WIDTH), F32)],
    )(gown, back, back_half)
    chip_sum, chip_half = call(
        chip_kernel, "chip", [whole()] * 2, [((BS, WIDTH), BF), ((HALF, WIDTH), BF)]
    )(device_sum, other_core(device_sum))
    chip_sum, dscore = lax.optimization_barrier((chip_sum, dscore))
    near = along_x(chip_sum, 1, 3)
    far = along_x(chip_half, 2, 2)
    dquery = pl.pallas_call(
        query_kernel,
        grid=(total // STEP,),
        in_specs=[whole()] * 5,
        out_specs=pl.BlockSpec((STEP // BS, WIDTH, BS), lambda t: (t, 0, 0)),
        out_shape=jax.ShapeDtypeStruct((heads, WIDTH, rows), BF),
        scratch_shapes=[pltpu.VMEM((KEYS, WIDTH), BF), pltpu.VMEM((WIDTH, KEYS), BF)],
        cost_estimate=pl.CostEstimate(flops=2 * total * KEYS * 768, bytes_accessed=4 * total * WIDTH, transcendentals=0),
        compiler_params=params,
        name="dquery",
    )(dscore, keys, mine, other, table)
    near, dquery = lax.optimization_barrier((near, dquery))
    rest = other_core(jnp.concatenate([near, far]))
    d_latent = pl.pallas_call(
        finish_kernel,
        in_specs=[whole()] * 5,
        out_specs=whole(),
        out_shape=jax.ShapeDtypeStruct((WIDTH, BS), BF),
        scratch_shapes=[pltpu.VMEM((BS, WIDTH), F32)],
        compiler_params=params,
        name="finish",
    )(*map(in_vmem, (chip_sum, near, far, rest, table)))
    return (dquery.transpose(2, 0, 1), d_latent.T)


def solution(mesh):
    placed = (P("cp", "tp", None), P("cp", None), P("cp", "tp", None), P("cp", None), P("cp"))
    return jax.shard_map(
        on_device,
        mesh=mesh,
        in_specs=placed,
        out_specs=(P("cp", "tp", None), P("cp", None)),
        check_vma=False,
    )
```

```python
import functools

import jax
import jax.numpy as jnp
import numpy as np
from jax import lax
from jax.experimental import pallas as pl
from jax.experimental.pallas import tpu as pltpu
from jax.sharding import PartitionSpec as P

LAT = 512
ROPE = 64
BS = 128
WIDTH = LAT + ROPE
HALF = BS // 2
SIDE = BS + HALF
REMOTE = 2 * SIDE
KEYS = BS + REMOTE
TILE = 256
STEP = 1024
EVEN, ODD, BOTH = 2, 3, 1

score_scale = 192.0 ** (-0.5)
rope_base = 10000.0
exponent_scale = score_scale * float(np.log2(np.e))
MASKED = -1e30

BF = jnp.bfloat16
F32 = jnp.float32
NT = (((1,), (1,)), ((), ()))
NN = (((1,), (0,)), ((), ()))
TN = (((0,), (0,)), ((), ()))


def dot(a, b, dims):
    return lax.dot_general(a, b, dims, preferred_element_type=F32)


def vmem(shape, dtype):
    return pltpu.VMEM(shape, dtype)


def in_vmem(x):
    return pltpu.with_memory_space_constraint(x, pltpu.VMEM)


def in_hbm(x):
    return pltpu.with_memory_space_constraint(x, pltpu.HBM)


def whole():
    return pl.BlockSpec(memory_space=pltpu.VMEM)


def scalars():
    return pl.BlockSpec(memory_space=pltpu.SMEM)


def turn(values, table):
    half = ROPE // 2
    first, second, cosine, sine = values[:half], values[half:], table[:half], table[half:]
    return jnp.concatenate([first * cosine - second * sine, first * sine + second * cosine], axis=0)


def turn_back(values, table):
    half = ROPE // 2
    first, second, cosine, sine = values[:half], values[half:], table[:half], table[half:]
    return jnp.concatenate([first * cosine + second * sine, second * cosine - first * sine], axis=0)


def heads_of(ref, first, count, rows=(0, WIDTH)):
    lo, hi = rows
    return jnp.concatenate([ref[h * WIDTH + lo : h * WIDTH + hi, :] for h in range(first, first + count)], axis=1)


def this_core():
    return lax.rem(lax.axis_index("tp"), 2)


def keys_kernel(anc_ref, parents_ref, freq_hbm, latent_hbm, grad_hbm,
                keys_ref, half_ref, table_ref, closure_ref, bias_ref, grad_ref, freq_ref, latent_ref, sems):
    first = grad_hbm.at[pl.ds(0, grad_ref.shape[0])]
    copies = [
        pltpu.make_async_copy(source, target, sems.at[k])
        for k, (source, target) in enumerate(((latent_hbm, latent_ref), (freq_hbm, freq_ref), (first, grad_ref)))
    ]
    for copy in copies:
        copy.start()
    row = lax.broadcasted_iota(jnp.int32, (BS, BS), 0)
    col = lax.broadcasted_iota(jnp.int32, (BS, BS), 1)
    linked = (row == parents_ref[...]) | (row == col)

    def sweep(closure):
        return jnp.minimum(dot(closure.astype(BF), closure.astype(BF), NN), 1.0)

    reach = jnp.where(linked, 1.0, 0.0)
    early = 4
    for _ in range(early):
        reach = sweep(reach)
    closure_ref[...] = reach

    @pl.when(jnp.max(jnp.sum(reach, axis=0, keepdims=True)) > 2.0**early)
    def _():
        deep = closure_ref[...]
        for _ in range((BS - 1).bit_length() - early):
            deep = sweep(deep)
        closure_ref[...] = deep

    depth = jnp.sum(closure_ref[...], axis=0, keepdims=True) - 1.0
    block, core = lax.axis_index("cp"), this_core()
    count = 0
    for k in range(anc_ref.shape[1]):
        count = count + (anc_ref[0, k] >= 0).astype(jnp.int32)

    def bias(offset):
        wanted = block - offset
        listed = jnp.int32(0)
        for k in range(anc_ref.shape[1]):
            listed = jnp.where(anc_ref[0, k] == wanted, 1, listed)
        return jnp.where((wanted >= 0) & (listed > 0), 0.0, MASKED).astype(F32)

    for k, offset in enumerate((EVEN + (ODD - EVEN) * core, BOTH, ODD - (ODD - EVEN) * core, BOTH)):
        bias_ref[k : k + 1, :] = jnp.full((1, TILE), bias(offset), F32)
    bias_ref[4:, :] = jnp.zeros((4, TILE), F32)
    copies[1].wait()
    angles = (depth + (BS * count).astype(F32)) * freq_ref[...]
    table = jnp.concatenate([jnp.cos(angles), jnp.sin(angles)], axis=0)
    table_ref[...] = table
    copies[0].wait()
    for lo in range(0, LAT, BS):
        keys_ref[:, lo : lo + BS] = latent_ref[lo : lo + BS, :].T
    turned = turn(latent_ref[LAT:, :].astype(F32), table)
    keys_ref[:, LAT:] = turned.T.astype(BF)
    half_ref[...] = keys_ref[own_half(), :]
    copies[2].wait()


def partial_softmax(score, slope, stat_ref, first, here):
    largest = jnp.max(score, axis=0, keepdims=True)
    expo = jnp.exp2(score - largest)
    stat_ref[first : first + 1, here] = largest
    stat_ref[first + 1 : first + 2, here] = jnp.sum(expo, axis=0, keepdims=True)
    stat_ref[first + 2 : first + 3, here] = jnp.sum(expo * slope, axis=0, keepdims=True)
    return expo


def own_kernel(heads, query_hbm, grad_hbm, early_ref, keys_ref, table_ref, closure_ref,
               query_ref, sorted_ref, expo_ref, slope_ref, stat_ref, late_ref, sems):
    per = TILE // BS
    pieces = heads // per
    pair = per * WIDTH
    late = late_ref.shape[0]
    grad_copy = pltpu.make_async_copy(grad_hbm.at[pl.ds(late, late)], late_ref, sems.at[pieces])
    grad_copy.start()
    copies = []
    for t in range(pieces):
        at = pl.ds(t * pair, pair)
        copies.append(pltpu.make_async_copy(query_hbm.at[at], query_ref.at[at], sems.at[t]))
    for copy in copies:
        copy.start()
    rows = TILE // heads
    row = lax.broadcasted_iota(jnp.int32, (TILE, TILE), 0)
    col = lax.broadcasted_iota(jnp.int32, (TILE, TILE), 1)
    order = jnp.where(col == (row % rows) * heads + row // rows, 1.0, 0.0).astype(BF)
    table = table_ref[...]
    seen = jnp.concatenate([closure_ref[...]] * per, axis=1) > 0.5
    for t in range(pieces):
        if t == pieces // 2:
            grad_copy.wait()
        source, at = (early_ref, t * TILE) if t < pieces // 2 else (late_ref, t * TILE - late)
        chunk = dot(order, source[at : at + TILE, :], NN).astype(BF)
        for h in range(heads):
            sorted_ref[pl.ds(h * BS + t * rows, rows), :] = chunk[h * rows : (h + 1) * rows]
    for copy in copies:
        copy.wait()
    for h in range(heads):
        tail = pl.ds(h * WIDTH + LAT, ROPE)
        query_ref[tail, :] = turn(query_ref[tail, :].astype(F32), table).astype(BF)
    for t in range(pieces):
        here = pl.ds(t * TILE, TILE)
        score = dot(keys_ref[...], heads_of(query_ref, per * t, per), NN)
        score = jnp.where(seen, score * exponent_scale, MASKED)
        slope = dot(keys_ref[:, :LAT], sorted_ref[here, :], NT)
        expo_ref[:, here] = partial_softmax(score, slope, stat_ref, 0, here)
        slope_ref[:, here] = slope


def key_grads(rows, weight_ref, dscore_ref, query_ref, sorted_ref):
    heads = query_ref.shape[0] // WIDTH
    turned = dot(dscore_ref[rows, :], heads_of(query_ref, 0, heads), NT) * score_scale
    plain = dot(weight_ref[rows, :], sorted_ref[...], NN)
    return turned[:, :LAT] + plain, turned[:, LAT:]


def mine_kernel(query_ref, sorted_ref, mine_ref, expo_ref, slope_ref, stat_ref):
    per = TILE // BS
    for t in range(sorted_ref.shape[0] // TILE):
        here = pl.ds(t * TILE, TILE)
        score = dot(mine_ref[...], heads_of(query_ref, per * t, per), NN) * exponent_scale
        slope = dot(mine_ref[:, :LAT], sorted_ref[here, :], NT)
        slope_ref[:, here] = slope
        expo_ref[:BS, here] = partial_softmax(score[:BS], slope[:BS], stat_ref, 0, here)
        expo_ref[BS:, here] = partial_softmax(score[BS:], slope[BS:], stat_ref, 3, here)


def main_kernel(bias_ref, query_ref, sorted_ref, other_ref, own_expo, own_slope, own_stat, mine_expo, mine_slope, mine_stat,
                weight_ref, dscore_ref, gother_ref, score_ref, slope_ref):
    tiles = sorted_ref.shape[0] // TILE
    per = TILE // BS
    whole_mine, part, whole_other, _ = (bias_ref[k : k + 1, :] for k in range(4))

    def products(t):
        here = pl.ds(t * TILE, TILE)
        score_ref[t % 2] = dot(other_ref[...], heads_of(query_ref, per * t, per), NN) * exponent_scale
        slope_ref[t % 2] = dot(other_ref[:, :LAT], sorted_ref[here, :], NT)

    def softmax(t):
        here = pl.ds(t * TILE, TILE)
        before = (
            (own_expo[:, here], own_slope[:, here], own_stat, 0, 0.0),
            (mine_expo[:BS, here], mine_slope[:BS, here], mine_stat, 0, whole_mine),
            (mine_expo[BS:, here], mine_slope[BS:, here], mine_stat, 3, part),
        )
        places = (
            (score_ref[t % 2, :BS], slope_ref[t % 2, :BS], whole_other),
            (score_ref[t % 2, BS:], slope_ref[t % 2, BS:], part),
        )
        tops = [stat[k : k + 1, here] + b for _, _, stat, k, b in before]
        largest = functools.reduce(
            jnp.maximum, tops + [jnp.max(s, axis=0, keepdims=True) + b for s, _, b in places]
        )
        factors = [jnp.exp2(top - largest) for top in tops]
        expos = [jnp.exp2(s - (largest - b)) for s, _, b in places]
        inverse = 1.0 / (
            sum(stat[k + 1 : k + 2, here] * f for (_, _, stat, k, _), f in zip(before, factors))
            + sum(jnp.sum(e, axis=0, keepdims=True) for e in expos)
        )
        delta = inverse * (
            sum(stat[k + 2 : k + 3, here] * f for (_, _, stat, k, _), f in zip(before, factors))
            + sum(jnp.sum(e * l, axis=0, keepdims=True) for e, (_, l, _) in zip(expos, places))
        )
        parts = [(e, l, f * inverse) for (e, l, _, _, _), f in zip(before, factors)]
        parts += [(e, l, inverse) for e, (_, l, _) in zip(expos, places)]
        at = 0
        for e, l, factor in parts:
            rows = pl.ds(at, e.shape[0])
            weight = e * factor
            weight_ref[rows, here] = weight.astype(BF)
            dscore_ref[rows, here] = (weight * (l - delta)).astype(BF)
            at += e.shape[0]

    products(0)
    for t in range(tiles):
        if t + 1 < tiles:
            products(t + 1)
        softmax(t)
    lead, tail = key_grads(pl.ds(BS + SIDE, SIDE), weight_ref, dscore_ref, query_ref, sorted_ref)
    gother_ref[:, :LAT] = lead.astype(BF)
    gother_ref[:, LAT:] = tail.astype(BF)


def grads_kernel(rows, weight_ref, dscore_ref, query_ref, sorted_ref, out_ref):
    lead, tail = key_grads(rows, weight_ref, dscore_ref, query_ref, sorted_ref)
    out_ref[:, :LAT] = lead
    out_ref[:, LAT:] = tail


def query_kernel(dscore_ref, keys_ref, mine_ref, other_ref, table_ref, dquery_ref, every_ref, turned_ref):
    t = pl.program_id(0)

    @pl.when(t == 0)
    def _():
        every_ref[:BS, :] = keys_ref[...]
        every_ref[BS : BS + SIDE, :] = mine_ref[...]
        every_ref[BS + SIDE :, :] = other_ref[...]
        for lo in range(0, KEYS, BS):
            turned_ref[:, lo : lo + BS] = every_ref[lo : lo + BS, :].T

    dscore = dscore_ref[:, pl.ds(pl.multiple_of(t * STEP, STEP), STEP)]
    grads = dot(turned_ref[...], dscore, NN) * score_scale
    for k in range(STEP // BS):
        part = grads[:, k * BS : (k + 1) * BS]
        dquery_ref[k, :LAT, :] = part[:LAT].astype(BF)
        dquery_ref[k, LAT:, :] = turn_back(part[LAT:], table_ref[...]).astype(BF)


def own_half():
    return pl.ds(pl.multiple_of(this_core() * HALF, HALF), HALF)


def other_half():
    return pl.ds(pl.multiple_of((1 - this_core()) * HALF, HALF), HALF)


def device_kernel(gown_ref, back_ref, half_ref, out_ref, sum_ref):
    sum_ref[...] = gown_ref[...] + back_ref[...].astype(F32)
    sum_ref[own_half(), :] += half_ref[...].astype(F32)
    out_ref[...] = sum_ref[...].astype(BF)


def chip_kernel(device_ref, other_ref, chip_ref, half_ref):
    chip_ref[...] = (device_ref[...].astype(F32) + other_ref[...].astype(F32)).astype(BF)
    half_ref[...] = chip_ref[own_half(), :]


def finish_kernel(chip_ref, near_ref, far_ref, rest_ref, table_ref, out_ref, sum_ref):
    sum_ref[...] = chip_ref[...].astype(F32)
    sum_ref[own_half(), :] += far_ref[...].astype(F32)
    sum_ref[other_half(), :] += rest_ref[BS:, :].astype(F32)
    sum_ref[...] += near_ref[...].astype(F32) + rest_ref[:BS, :].astype(F32)
    for lo in range(0, LAT, BS):
        out_ref[lo : lo + BS, :] = sum_ref[:, lo : lo + BS].T.astype(BF)
    out_ref[LAT:, :] = turn_back(sum_ref[:, LAT:].T, table_ref[...]).astype(BF)


def by_core(block, even, odd):
    tp, cp = lax.axis_size("tp"), lax.axis_size("cp")
    route = []
    for t in range(tp):
        step = odd if t % 2 else even
        for c in range(cp):
            if 0 <= c + step < cp or WRAP:
                route.append((t * cp + c, t * cp + (c + step) % cp))
    return lax.ppermute(block, ("tp", "cp"), route)


WRAP = True


def other_core(block):
    return lax.ppermute(block, "tp", [(t, t ^ 1) for t in range(lax.axis_size("tp"))])


def along_x(block, even, odd):
    route = [(t, t ^ (2 * (odd if t % 2 else even))) for t in range(lax.axis_size("tp"))]
    return lax.ppermute(block, "tp", route)


def on_device(query, latent, grad_out, ancestors, parents):
    rows, heads, _ = query.shape
    total = rows * heads
    half = ROPE // 2
    lane_freq = rope_base ** (-2.0 * np.arange(half, dtype=np.float64) / ROPE)
    freq = jnp.asarray(np.tile(lane_freq[:, None], (1, BS)), dtype=F32)
    params = pltpu.CompilerParams(vmem_limit_bytes=16 * 2**20)
    outside = pl.BlockSpec(memory_space=pltpu.HBM)

    def call(kernel, name, ins, outs, flops=0, **more):
        return pl.pallas_call(
            kernel,
            in_specs=ins,
            out_specs=[whole()] * len(outs),
            out_shape=[vmem(*o) for o in outs],
            cost_estimate=pl.CostEstimate(flops=flops, bytes_accessed=4 * total * WIDTH, transcendentals=0),
            compiler_params=params,
            name=name,
            **more,
        )

    keys, keys_half, table, closure, bias, early = call(
        keys_kernel,
        "keys",
        [scalars(), whole(), outside, outside, outside],
        [((BS, WIDTH), BF), ((HALF, WIDTH), BF), ((ROPE, BS), F32), ((BS, BS), F32), ((8, TILE), F32), ((total // 2, LAT), BF)],
        scratch_shapes=[pltpu.VMEM((half, BS), F32), pltpu.VMEM((WIDTH, BS), BF), pltpu.SemaphoreType.DMA((3,))],
    )(*map(in_hbm, (ancestors, parents.reshape(1, BS), freq, latent.T, grad_out.reshape(total, LAT))))

    fetched = by_core(keys, EVEN, ODD)
    fetched_half = by_core(keys_half, BOTH, BOTH)

    q, g, own_expo, own_slope, own_stat = call(
        functools.partial(own_kernel, heads),
        "own",
        [outside] * 2 + [whole()] * 4,
        [((heads * WIDTH, rows), BF), ((total, LAT), BF), ((BS, total), F32), ((BS, total), F32), ((8, total), F32)],
        flops=2 * total * BS * 1800,
        scratch_shapes=[pltpu.VMEM((total // 2, LAT), BF), pltpu.SemaphoreType.DMA((total // TILE + 1,))],
    )(in_hbm(query.transpose(1, 2, 0).reshape(heads * WIDTH, rows)), in_hbm(grad_out.reshape(total, LAT)),
      early, keys, table, closure)

    mine, q = lax.optimization_barrier((jnp.concatenate([fetched, fetched_half]), q))
    other = other_core(mine)
    mine_expo, mine_slope, mine_stat = call(
        mine_kernel,
        "mine",
        [whole()] * 3,
        [((SIDE, total), F32), ((SIDE, total), F32), ((8, total), F32)],
        flops=2 * total * SIDE * 1280,
    )(q, g, mine)

    weight, dscore, gother = call(
        main_kernel,
        "main",
        [whole()] * 10,
        [((KEYS, total), BF), ((KEYS, total), BF), ((SIDE, WIDTH), BF)],
        flops=2 * total * SIDE * 2560,
        scratch_shapes=[pltpu.VMEM((2, SIDE, TILE), F32), pltpu.VMEM((2, SIDE, TILE), F32)],
    )(bias, q, g, other, own_expo, own_slope, own_stat, mine_expo, mine_slope, mine_stat)

    gother = other_core(gother)
    (gmine,) = call(
        functools.partial(grads_kernel, slice(BS, BS + SIDE)),
        "grads",
        [whole()] * 4,
        [((SIDE, WIDTH), F32)],
        flops=2 * total * SIDE * 1280,
    )(weight, dscore, q, g)
    gmine = (gmine + gother.astype(F32)).astype(BF)
    back = by_core(gmine[:BS], -EVEN, -ODD)
    back_half = by_core(gmine[BS:], -BOTH, -BOTH)

    (gown,) = call(
        functools.partial(grads_kernel, slice(0, BS)),
        "gown",
        [whole()] * 4,
        [((BS, WIDTH), F32)],
        flops=2 * total * BS * 1280,
    )(weight, dscore, q, g)
    (device_sum,) = call(
        device_kernel,
        "device",
        [whole()] * 3,
        [((BS, WIDTH), BF)],
        scratch_shapes=[pltpu.VMEM((BS, WIDTH), F32)],
    )(gown, back, back_half)
    chip_sum, chip_half = call(
        chip_kernel, "chip", [whole()] * 2, [((BS, WIDTH), BF), ((HALF, WIDTH), BF)]
    )(device_sum, other_core(device_sum))
    chip_sum, dscore = lax.optimization_barrier((chip_sum, dscore))
    near = along_x(chip_sum, 1, 3)
    far = along_x(chip_half, 2, 2)
    dquery = pl.pallas_call(
        query_kernel,
        grid=(total // STEP,),
        in_specs=[whole()] * 5,
        out_specs=pl.BlockSpec((STEP // BS, WIDTH, BS), lambda t: (t, 0, 0)),
        out_shape=jax.ShapeDtypeStruct((heads, WIDTH, rows), BF),
        scratch_shapes=[pltpu.VMEM((KEYS, WIDTH), BF), pltpu.VMEM((WIDTH, KEYS), BF)],
        cost_estimate=pl.CostEstimate(flops=2 * total * KEYS * 768, bytes_accessed=4 * total * WIDTH, transcendentals=0),
        compiler_params=params,
        name="dquery",
    )(dscore, keys, mine, other, table)
    near, dquery = lax.optimization_barrier((near, dquery))
    rest = other_core(jnp.concatenate([near, far]))
    d_latent = pl.pallas_call(
        finish_kernel,
        in_specs=[whole()] * 5,
        out_specs=whole(),
        out_shape=jax.ShapeDtypeStruct((WIDTH, BS), BF),
        scratch_shapes=[pltpu.VMEM((BS, WIDTH), F32)],
        compiler_params=params,
        name="finish",
    )(*map(in_vmem, (chip_sum, near, far, rest, table)))
    return (dquery.transpose(2, 0, 1), d_latent.T)


def solution(mesh):
    placed = (P("cp", "tp", None), P("cp", None), P("cp", "tp", None), P("cp", None), P("cp"))
    return jax.shard_map(
        on_device,
        mesh=mesh,
        in_specs=placed,
        out_specs=(P("cp", "tp", None), P("cp", None)),
        check_vma=False,
    )
```

```python
import functools

import jax
import jax.numpy as jnp
import numpy as np
from jax import lax
from jax.experimental import pallas as pl
from jax.experimental.pallas import tpu as pltpu
from jax.sharding import PartitionSpec as P

LAT = 512
ROPE = 64
BS = 128
WIDTH = LAT + ROPE
HALF = BS // 2
SIDE = BS + HALF
REMOTE = 2 * SIDE
KEYS = BS + REMOTE
TILE = 256
STEP = 1024
EVEN, ODD, BOTH = 2, 3, 1

score_scale = 192.0 ** (-0.5)
rope_base = 10000.0
exponent_scale = score_scale * float(np.log2(np.e))
MASKED = -1e30

BF = jnp.bfloat16
F32 = jnp.float32
NT = (((1,), (1,)), ((), ()))
NN = (((1,), (0,)), ((), ()))
TN = (((0,), (0,)), ((), ()))


def dot(a, b, dims):
    return lax.dot_general(a, b, dims, preferred_element_type=F32)


def vmem(shape, dtype):
    return pltpu.VMEM(shape, dtype)


def in_vmem(x):
    return pltpu.with_memory_space_constraint(x, pltpu.VMEM)


def in_hbm(x):
    return pltpu.with_memory_space_constraint(x, pltpu.HBM)


def whole():
    return pl.BlockSpec(memory_space=pltpu.VMEM)


def scalars():
    return pl.BlockSpec(memory_space=pltpu.SMEM)


def turn(values, table):
    half = ROPE // 2
    first, second, cosine, sine = values[:half], values[half:], table[:half], table[half:]
    return jnp.concatenate([first * cosine - second * sine, first * sine + second * cosine], axis=0)


def turn_back(values, table):
    half = ROPE // 2
    first, second, cosine, sine = values[:half], values[half:], table[:half], table[half:]
    return jnp.concatenate([first * cosine + second * sine, second * cosine - first * sine], axis=0)


def heads_of(ref, first, count, rows=(0, WIDTH)):
    lo, hi = rows
    return jnp.concatenate([ref[h * WIDTH + lo : h * WIDTH + hi, :] for h in range(first, first + count)], axis=1)


def this_core():
    return lax.rem(lax.axis_index("tp"), 2)


def keys_kernel(anc_ref, parents_ref, freq_hbm, latent_hbm, grad_hbm,
                keys_ref, half_ref, table_ref, closure_ref, bias_ref, grad_ref, freq_ref, latent_ref, sems):
    first = grad_hbm.at[pl.ds(0, grad_ref.shape[0])]
    copies = [
        pltpu.make_async_copy(source, target, sems.at[k])
        for k, (source, target) in enumerate(((latent_hbm, latent_ref), (freq_hbm, freq_ref), (first, grad_ref)))
    ]
    for copy in copies:
        copy.start()
    row = lax.broadcasted_iota(jnp.int32, (BS, BS), 0)
    col = lax.broadcasted_iota(jnp.int32, (BS, BS), 1)
    linked = (row == parents_ref[...]) | (row == col)

    def sweep(closure):
        return jnp.minimum(dot(closure.astype(BF), closure.astype(BF), NN), 1.0)

    reach = jnp.where(linked, 1.0, 0.0)
    early = 4
    for _ in range(early):
        reach = sweep(reach)
    closure_ref[...] = reach

    @pl.when(jnp.max(jnp.sum(reach, axis=0, keepdims=True)) > 2.0**early)
    def _():
        deep = closure_ref[...]
        for _ in range((BS - 1).bit_length() - early):
            deep = sweep(deep)
        closure_ref[...] = deep

    depth = jnp.sum(closure_ref[...], axis=0, keepdims=True) - 1.0
    block, core = lax.axis_index("cp"), this_core()
    count = 0
    for k in range(anc_ref.shape[1]):
        count = count + (anc_ref[0, k] >= 0).astype(jnp.int32)

    def bias(offset):
        wanted = block - offset
        listed = jnp.int32(0)
        for k in range(anc_ref.shape[1]):
            listed = jnp.where(anc_ref[0, k] == wanted, 1, listed)
        return jnp.where((wanted >= 0) & (listed > 0), 0.0, MASKED).astype(F32)

    for k, offset in enumerate((EVEN + (ODD - EVEN) * core, BOTH, ODD - (ODD - EVEN) * core, BOTH)):
        bias_ref[k : k + 1, :] = jnp.full((1, TILE), bias(offset), F32)
    bias_ref[4:, :] = jnp.zeros((4, TILE), F32)
    copies[1].wait()
    angles = (depth + (BS * count).astype(F32)) * freq_ref[...]
    table = jnp.concatenate([jnp.cos(angles), jnp.sin(angles)], axis=0)
    table_ref[...] = table
    copies[0].wait()
    for lo in range(0, LAT, BS):
        keys_ref[:, lo : lo + BS] = latent_ref[lo : lo + BS, :].T
    turned = turn(latent_ref[LAT:, :].astype(F32), table)
    keys_ref[:, LAT:] = turned.T.astype(BF)
    half_ref[...] = keys_ref[own_half(), :]
    copies[2].wait()


def partial_softmax(score, slope, stat_ref, first, here):
    largest = jnp.max(score, axis=0, keepdims=True)
    expo = jnp.exp2(score - largest)
    stat_ref[first : first + 1, here] = largest
    stat_ref[first + 1 : first + 2, here] = jnp.sum(expo, axis=0, keepdims=True)
    stat_ref[first + 2 : first + 3, here] = jnp.sum(expo * slope, axis=0, keepdims=True)
    return expo


def own_kernel(heads, query_hbm, grad_hbm, early_ref, keys_ref, table_ref, closure_ref,
               query_ref, sorted_ref, expo_ref, slope_ref, stat_ref, late_ref, sems):
    per = TILE // BS
    pieces = heads // per
    pair = per * WIDTH
    early, late = early_ref.shape[0], late_ref.shape[0]
    grad_copy = pltpu.make_async_copy(grad_hbm.at[pl.ds(early, late)], late_ref, sems.at[pieces])
    grad_copy.start()
    copies = []
    for t in range(pieces):
        at = pl.ds(t * pair, pair)
        copies.append(pltpu.make_async_copy(query_hbm.at[at], query_ref.at[at], sems.at[t]))
    for copy in copies:
        copy.start()
    rows = TILE // heads
    row = lax.broadcasted_iota(jnp.int32, (TILE, TILE), 0)
    col = lax.broadcasted_iota(jnp.int32, (TILE, TILE), 1)
    order = jnp.where(col == (row % rows) * heads + row // rows, 1.0, 0.0).astype(BF)
    table = table_ref[...]
    seen = jnp.concatenate([closure_ref[...]] * per, axis=1) > 0.5
    for t in range(pieces):
        if t * TILE == early:
            grad_copy.wait()
        source, at = (early_ref, t * TILE) if t * TILE < early else (late_ref, t * TILE - early)
        chunk = dot(order, source[at : at + TILE, :], NN).astype(BF)
        for h in range(heads):
            sorted_ref[pl.ds(h * BS + t * rows, rows), :] = chunk[h * rows : (h + 1) * rows]
    for copy in copies:
        copy.wait()
    for h in range(heads):
        tail = pl.ds(h * WIDTH + LAT, ROPE)
        query_ref[tail, :] = turn(query_ref[tail, :].astype(F32), table).astype(BF)
    for t in range(pieces):
        here = pl.ds(t * TILE, TILE)
        score = dot(keys_ref[...], heads_of(query_ref, per * t, per), NN)
        score = jnp.where(seen, score * exponent_scale, MASKED)
        slope = dot(keys_ref[:, :LAT], sorted_ref[here, :], NT)
        expo_ref[:, here] = partial_softmax(score, slope, stat_ref, 0, here)
        slope_ref[:, here] = slope


def key_grads(rows, weight_ref, dscore_ref, query_ref, sorted_ref):
    heads = query_ref.shape[0] // WIDTH
    turned = dot(dscore_ref[rows, :], heads_of(query_ref, 0, heads), NT) * score_scale
    plain = dot(weight_ref[rows, :], sorted_ref[...], NN)
    return turned[:, :LAT] + plain, turned[:, LAT:]


def has_earlier():
    return lax.axis_index("cp") > 0


def mine_kernel(query_ref, sorted_ref, mine_ref, expo_ref, slope_ref, stat_ref):
    per = TILE // BS

    @pl.when(has_earlier())
    def _():
        for t in range(sorted_ref.shape[0] // TILE):
            here = pl.ds(t * TILE, TILE)
            score = dot(mine_ref[...], heads_of(query_ref, per * t, per), NN) * exponent_scale
            slope = dot(mine_ref[:, :LAT], sorted_ref[here, :], NT)
            slope_ref[:, here] = slope
            expo_ref[:BS, here] = partial_softmax(score[:BS], slope[:BS], stat_ref, 0, here)
            expo_ref[BS:, here] = partial_softmax(score[BS:], slope[BS:], stat_ref, 3, here)


def main_kernel(bias_ref, query_ref, sorted_ref, other_ref, own_expo, own_slope, own_stat, mine_expo, mine_slope, mine_stat,
                weight_ref, dscore_ref, gother_ref, score_ref, slope_ref):
    tiles = sorted_ref.shape[0] // TILE
    per = TILE // BS
    whole_mine, part, whole_other, _ = (bias_ref[k : k + 1, :] for k in range(4))

    def products(t):
        here = pl.ds(t * TILE, TILE)
        score_ref[t % 2] = dot(other_ref[...], heads_of(query_ref, per * t, per), NN) * exponent_scale
        slope_ref[t % 2] = dot(other_ref[:, :LAT], sorted_ref[here, :], NT)

    def softmax(t, remote):
        here = pl.ds(t * TILE, TILE)
        before = (
            (own_expo[:, here], own_slope[:, here], own_stat, 0, 0.0),
            (mine_expo[:BS, here], mine_slope[:BS, here], mine_stat, 0, whole_mine),
            (mine_expo[BS:, here], mine_slope[BS:, here], mine_stat, 3, part),
        )
        places = (
            (score_ref[t % 2, :BS], slope_ref[t % 2, :BS], whole_other),
            (score_ref[t % 2, BS:], slope_ref[t % 2, BS:], part),
        )
        if not remote:
            before, places = before[:1], ()
        tops = [stat[k : k + 1, here] + b for _, _, stat, k, b in before]
        largest = functools.reduce(
            jnp.maximum, tops + [jnp.max(s, axis=0, keepdims=True) + b for s, _, b in places]
        )
        factors = [jnp.exp2(top - largest) for top in tops]
        expos = [jnp.exp2(s - (largest - b)) for s, _, b in places]
        inverse = 1.0 / (
            sum(stat[k + 1 : k + 2, here] * f for (_, _, stat, k, _), f in zip(before, factors))
            + sum(jnp.sum(e, axis=0, keepdims=True) for e in expos)
        )
        delta = inverse * (
            sum(stat[k + 2 : k + 3, here] * f for (_, _, stat, k, _), f in zip(before, factors))
            + sum(jnp.sum(e * l, axis=0, keepdims=True) for e, (_, l, _) in zip(expos, places))
        )
        parts = [(e, l, f * inverse) for (e, l, _, _, _), f in zip(before, factors)]
        parts += [(e, l, inverse) for e, (_, l, _) in zip(expos, places)]
        at = 0
        for e, l, factor in parts:
            rows = pl.ds(at, e.shape[0])
            weight = e * factor
            weight_ref[rows, here] = weight.astype(BF)
            dscore_ref[rows, here] = (weight * (l - delta)).astype(BF)
            at += e.shape[0]

    @pl.when(has_earlier())
    def _():
        products(0)
        for t in range(tiles):
            if t + 1 < tiles:
                products(t + 1)
            softmax(t, True)
        lead, tail = key_grads(pl.ds(BS + SIDE, SIDE), weight_ref, dscore_ref, query_ref, sorted_ref)
        gother_ref[:, :LAT] = lead.astype(BF)
        gother_ref[:, LAT:] = tail.astype(BF)

    @pl.when(jnp.logical_not(has_earlier()))
    def _():
        for t in range(tiles):
            softmax(t, False)
        weight_ref[BS:, :] = jnp.zeros((REMOTE, weight_ref.shape[1]), BF)
        dscore_ref[BS:, :] = jnp.zeros((REMOTE, dscore_ref.shape[1]), BF)
        gother_ref[...] = jnp.zeros_like(gother_ref)


def mine_grads_kernel(weight_ref, dscore_ref, query_ref, sorted_ref, out_ref):
    @pl.when(has_earlier())
    def _():
        grads_kernel(slice(BS, BS + SIDE), weight_ref, dscore_ref, query_ref, sorted_ref, out_ref)

    @pl.when(jnp.logical_not(has_earlier()))
    def _():
        out_ref[...] = jnp.zeros_like(out_ref)


def grads_kernel(rows, weight_ref, dscore_ref, query_ref, sorted_ref, out_ref):
    lead, tail = key_grads(rows, weight_ref, dscore_ref, query_ref, sorted_ref)
    out_ref[:, :LAT] = lead
    out_ref[:, LAT:] = tail


def query_kernel(dscore_ref, keys_ref, mine_ref, other_ref, table_ref, dquery_ref, every_ref, turned_ref):
    t = pl.program_id(0)

    @pl.when(t == 0)
    def _():
        every_ref[:BS, :] = keys_ref[...]
        every_ref[BS : BS + SIDE, :] = mine_ref[...]
        every_ref[BS + SIDE :, :] = other_ref[...]
        for lo in range(0, KEYS, BS):
            turned_ref[:, lo : lo + BS] = every_ref[lo : lo + BS, :].T

    dscore = dscore_ref[:, pl.ds(pl.multiple_of(t * STEP, STEP), STEP)]
    grads = dot(turned_ref[...], dscore, NN) * score_scale
    for k in range(STEP // BS):
        part = grads[:, k * BS : (k + 1) * BS]
        dquery_ref[k, :LAT, :] = part[:LAT].astype(BF)
        dquery_ref[k, LAT:, :] = turn_back(part[LAT:], table_ref[...]).astype(BF)


def own_half():
    return pl.ds(pl.multiple_of(this_core() * HALF, HALF), HALF)


def other_half():
    return pl.ds(pl.multiple_of((1 - this_core()) * HALF, HALF), HALF)


def device_kernel(gown_ref, back_ref, half_ref, out_ref, sum_ref):
    sum_ref[...] = gown_ref[...] + back_ref[...].astype(F32)
    sum_ref[own_half(), :] += half_ref[...].astype(F32)
    out_ref[...] = sum_ref[...].astype(BF)


def chip_kernel(device_ref, other_ref, chip_ref, half_ref):
    chip_ref[...] = (device_ref[...].astype(F32) + other_ref[...].astype(F32)).astype(BF)
    half_ref[...] = chip_ref[own_half(), :]


def finish_kernel(chip_ref, near_ref, far_ref, rest_ref, table_ref, out_ref, sum_ref):
    sum_ref[...] = chip_ref[...].astype(F32)
    sum_ref[own_half(), :] += far_ref[...].astype(F32)
    sum_ref[other_half(), :] += rest_ref[BS:, :].astype(F32)
    sum_ref[...] += near_ref[...].astype(F32) + rest_ref[:BS, :].astype(F32)
    for lo in range(0, LAT, BS):
        out_ref[lo : lo + BS, :] = sum_ref[:, lo : lo + BS].T.astype(BF)
    out_ref[LAT:, :] = turn_back(sum_ref[:, LAT:].T, table_ref[...]).astype(BF)


def by_core(block, even, odd):
    tp, cp = lax.axis_size("tp"), lax.axis_size("cp")
    route = []
    for t in range(tp):
        step = odd if t % 2 else even
        for c in range(cp):
            if 0 <= c + step < cp or WRAP:
                route.append((t * cp + c, t * cp + (c + step) % cp))
    return lax.ppermute(block, ("tp", "cp"), route)


WRAP = True


def other_core(block):
    return lax.ppermute(block, "tp", [(t, t ^ 1) for t in range(lax.axis_size("tp"))])


def along_x(block, even, odd):
    route = [(t, t ^ (2 * (odd if t % 2 else even))) for t in range(lax.axis_size("tp"))]
    return lax.ppermute(block, "tp", route)


def on_device(query, latent, grad_out, ancestors, parents):
    rows, heads, _ = query.shape
    total = rows * heads
    half = ROPE // 2
    lane_freq = rope_base ** (-2.0 * np.arange(half, dtype=np.float64) / ROPE)
    freq = jnp.asarray(np.tile(lane_freq[:, None], (1, BS)), dtype=F32)
    params = pltpu.CompilerParams(vmem_limit_bytes=16 * 2**20)
    outside = pl.BlockSpec(memory_space=pltpu.HBM)

    def call(kernel, name, ins, outs, flops=0, **more):
        return pl.pallas_call(
            kernel,
            in_specs=ins,
            out_specs=[whole()] * len(outs),
            out_shape=[vmem(*o) for o in outs],
            cost_estimate=pl.CostEstimate(flops=flops, bytes_accessed=4 * total * WIDTH, transcendentals=0),
            compiler_params=params,
            name=name,
            **more,
        )

    keys, keys_half, table, closure, bias, early = call(
        keys_kernel,
        "keys",
        [scalars(), whole(), outside, outside, outside],
        [((BS, WIDTH), BF), ((HALF, WIDTH), BF), ((ROPE, BS), F32), ((BS, BS), F32), ((8, TILE), F32), ((total // 4, LAT), BF)],
        scratch_shapes=[pltpu.VMEM((half, BS), F32), pltpu.VMEM((WIDTH, BS), BF), pltpu.SemaphoreType.DMA((3,))],
    )(*map(in_hbm, (ancestors, parents.reshape(1, BS), freq, latent.T, grad_out.reshape(total, LAT))))

    fetched = by_core(keys, EVEN, ODD)
    fetched_half = by_core(keys_half, BOTH, BOTH)

    q, g, own_expo, own_slope, own_stat = call(
        functools.partial(own_kernel, heads),
        "own",
        [outside] * 2 + [whole()] * 4,
        [((heads * WIDTH, rows), BF), ((total, LAT), BF), ((BS, total), F32), ((BS, total), F32), ((8, total), F32)],
        flops=2 * total * BS * 1800,
        scratch_shapes=[pltpu.VMEM((total - total // 4, LAT), BF), pltpu.SemaphoreType.DMA((total // TILE + 1,))],
    )(in_hbm(query.transpose(1, 2, 0).reshape(heads * WIDTH, rows)), in_hbm(grad_out.reshape(total, LAT)),
      early, keys, table, closure)

    mine, q = lax.optimization_barrier((jnp.concatenate([fetched, fetched_half]), q))
    other = other_core(mine)
    mine_expo, mine_slope, mine_stat = call(
        mine_kernel,
        "mine",
        [whole()] * 3,
        [((SIDE, total), F32), ((SIDE, total), F32), ((8, total), F32)],
        flops=2 * total * SIDE * 1280,
    )(q, g, mine)

    weight, dscore, gother = call(
        main_kernel,
        "main",
        [whole()] * 10,
        [((KEYS, total), BF), ((KEYS, total), BF), ((SIDE, WIDTH), BF)],
        flops=2 * total * SIDE * 2560,
        scratch_shapes=[pltpu.VMEM((2, SIDE, TILE), F32), pltpu.VMEM((2, SIDE, TILE), F32)],
    )(bias, q, g, other, own_expo, own_slope, own_stat, mine_expo, mine_slope, mine_stat)

    gother = other_core(gother)
    (gmine,) = call(
        mine_grads_kernel,
        "grads",
        [whole()] * 4,
        [((SIDE, WIDTH), F32)],
        flops=2 * total * SIDE * 1280,
    )(weight, dscore, q, g)
    gmine = (gmine + gother.astype(F32)).astype(BF)
    back = by_core(gmine[:BS], -EVEN, -ODD)
    back_half = by_core(gmine[BS:], -BOTH, -BOTH)

    (gown,) = call(
        functools.partial(grads_kernel, slice(0, BS)),
        "gown",
        [whole()] * 4,
        [((BS, WIDTH), F32)],
        flops=2 * total * BS * 1280,
    )(weight, dscore, q, g)
    (device_sum,) = call(
        device_kernel,
        "device",
        [whole()] * 3,
        [((BS, WIDTH), BF)],
        scratch_shapes=[pltpu.VMEM((BS, WIDTH), F32)],
    )(gown, back, back_half)
    chip_sum, chip_half = call(
        chip_kernel, "chip", [whole()] * 2, [((BS, WIDTH), BF), ((HALF, WIDTH), BF)]
    )(device_sum, other_core(device_sum))
    chip_sum, dscore = lax.optimization_barrier((chip_sum, dscore))
    near = along_x(chip_sum, 1, 3)
    far = along_x(chip_half, 2, 2)
    dquery = pl.pallas_call(
        query_kernel,
        grid=(total // STEP,),
        in_specs=[whole()] * 5,
        out_specs=pl.BlockSpec((STEP // BS, WIDTH, BS), lambda t: (t, 0, 0)),
        out_shape=jax.ShapeDtypeStruct((heads, WIDTH, rows), BF),
        scratch_shapes=[pltpu.VMEM((KEYS, WIDTH), BF), pltpu.VMEM((WIDTH, KEYS), BF)],
        cost_estimate=pl.CostEstimate(flops=2 * total * KEYS * 768, bytes_accessed=4 * total * WIDTH, transcendentals=0),
        compiler_params=params,
        name="dquery",
    )(dscore, keys, mine, other, table)
    near, dquery = lax.optimization_barrier((near, dquery))
    rest = other_core(jnp.concatenate([near, far]))
    d_latent = pl.pallas_call(
        finish_kernel,
        in_specs=[whole()] * 5,
        out_specs=whole(),
        out_shape=jax.ShapeDtypeStruct((WIDTH, BS), BF),
        scratch_shapes=[pltpu.VMEM((BS, WIDTH), F32)],
        compiler_params=params,
        name="finish",
    )(*map(in_vmem, (chip_sum, near, far, rest, table)))
    return (dquery.transpose(2, 0, 1), d_latent.T)


def solution(mesh):
    placed = (P("cp", "tp", None), P("cp", None), P("cp", "tp", None), P("cp", None), P("cp"))
    return jax.shard_map(
        on_device,
        mesh=mesh,
        in_specs=placed,
        out_specs=(P("cp", "tp", None), P("cp", None)),
        check_vma=False,
    )
```

```python
import functools

import jax
import jax.numpy as jnp
import numpy as np
from jax import lax
from jax.experimental import pallas as pl
from jax.experimental.pallas import tpu as pltpu
from jax.sharding import PartitionSpec as P

LAT = 512
ROPE = 64
BS = 128
WIDTH = LAT + ROPE
HALF = BS // 2
SIDE = BS + HALF
REMOTE = 2 * SIDE
KEYS = BS + REMOTE
TILE = 256
STEP = 1024
EVEN, ODD, BOTH = 2, 3, 1

score_scale = 192.0 ** (-0.5)
rope_base = 10000.0
exponent_scale = score_scale * float(np.log2(np.e))
MASKED = -1e30

BF = jnp.bfloat16
F32 = jnp.float32
NT = (((1,), (1,)), ((), ()))
NN = (((1,), (0,)), ((), ()))
TN = (((0,), (0,)), ((), ()))


def dot(a, b, dims):
    return lax.dot_general(a, b, dims, preferred_element_type=F32)


def vmem(shape, dtype):
    return pltpu.VMEM(shape, dtype)


def in_vmem(x):
    return pltpu.with_memory_space_constraint(x, pltpu.VMEM)


def in_hbm(x):
    return pltpu.with_memory_space_constraint(x, pltpu.HBM)


def whole():
    return pl.BlockSpec(memory_space=pltpu.VMEM)


def scalars():
    return pl.BlockSpec(memory_space=pltpu.SMEM)


def turn(values, table):
    half = ROPE // 2
    first, second, cosine, sine = values[:half], values[half:], table[:half], table[half:]
    return jnp.concatenate([first * cosine - second * sine, first * sine + second * cosine], axis=0)


def turn_back(values, table):
    half = ROPE // 2
    first, second, cosine, sine = values[:half], values[half:], table[:half], table[half:]
    return jnp.concatenate([first * cosine + second * sine, second * cosine - first * sine], axis=0)


def heads_of(ref, first, count, rows=(0, WIDTH)):
    lo, hi = rows
    return jnp.concatenate([ref[h * WIDTH + lo : h * WIDTH + hi, :] for h in range(first, first + count)], axis=1)


def this_core():
    return lax.rem(lax.axis_index("tp"), 2)


def keys_kernel(anc_ref, parents_ref, freq_hbm, latent_hbm, grad_hbm,
                keys_ref, half_ref, table_ref, closure_ref, bias_ref, grad_ref, freq_ref, latent_ref, sems):
    first = grad_hbm.at[pl.ds(0, grad_ref.shape[0])]
    copies = [
        pltpu.make_async_copy(source, target, sems.at[k])
        for k, (source, target) in enumerate(((latent_hbm, latent_ref), (freq_hbm, freq_ref), (first, grad_ref)))
    ]
    for copy in copies:
        copy.start()
    row = lax.broadcasted_iota(jnp.int32, (BS, BS), 0)
    col = lax.broadcasted_iota(jnp.int32, (BS, BS), 1)
    linked = (row == parents_ref[...]) | (row == col)

    def sweep(closure):
        return jnp.minimum(dot(closure.astype(BF), closure.astype(BF), NN), 1.0)

    reach = jnp.where(linked, 1.0, 0.0)
    early = 4
    for _ in range(early):
        reach = sweep(reach)
    closure_ref[...] = reach

    @pl.when(jnp.max(jnp.sum(reach, axis=0, keepdims=True)) > 2.0**early)
    def _():
        deep = closure_ref[...]
        for _ in range((BS - 1).bit_length() - early):
            deep = sweep(deep)
        closure_ref[...] = deep

    depth = jnp.sum(closure_ref[...], axis=0, keepdims=True) - 1.0
    block, core = lax.axis_index("cp"), this_core()
    count = 0
    for k in range(anc_ref.shape[1]):
        count = count + (anc_ref[0, k] >= 0).astype(jnp.int32)

    def bias(offset):
        wanted = block - offset
        listed = jnp.int32(0)
        for k in range(anc_ref.shape[1]):
            listed = jnp.where(anc_ref[0, k] == wanted, 1, listed)
        return jnp.where((wanted >= 0) & (listed > 0), 0.0, MASKED).astype(F32)

    for k, offset in enumerate((EVEN + (ODD - EVEN) * core, BOTH, ODD - (ODD - EVEN) * core, BOTH)):
        bias_ref[k : k + 1, :] = jnp.full((1, TILE), bias(offset), F32)
    bias_ref[4:, :] = jnp.zeros((4, TILE), F32)
    copies[1].wait()
    angles = (depth + (BS * count).astype(F32)) * freq_ref[...]
    table = jnp.concatenate([jnp.cos(angles), jnp.sin(angles)], axis=0)
    table_ref[...] = table
    copies[0].wait()
    for lo in range(0, LAT, BS):
        keys_ref[:, lo : lo + BS] = latent_ref[lo : lo + BS, :].T
    turned = turn(latent_ref[LAT:, :].astype(F32), table)
    keys_ref[:, LAT:] = turned.T.astype(BF)
    half_ref[...] = keys_ref[own_half(), :]
    copies[2].wait()


def partial_softmax(score, slope, stat_ref, first, here):
    largest = jnp.max(score, axis=0, keepdims=True)
    expo = jnp.exp2(score - largest)
    stat_ref[first : first + 1, here] = largest
    stat_ref[first + 1 : first + 2, here] = jnp.sum(expo, axis=0, keepdims=True)
    stat_ref[first + 2 : first + 3, here] = jnp.sum(expo * slope, axis=0, keepdims=True)
    return expo


def own_kernel(heads, query_hbm, grad_hbm, early_ref, keys_ref, table_ref, closure_ref,
               query_ref, sorted_ref, expo_ref, slope_ref, stat_ref, late_ref, sems):
    per = TILE // BS
    pieces = heads // per
    pair = per * WIDTH
    early, late = early_ref.shape[0], late_ref.shape[0]
    grad_copy = pltpu.make_async_copy(grad_hbm.at[pl.ds(early, late)], late_ref, sems.at[pieces])
    grad_copy.start()
    copies = []
    for t in range(pieces):
        at = pl.ds(t * pair, pair)
        copies.append(pltpu.make_async_copy(query_hbm.at[at], query_ref.at[at], sems.at[t]))
    for copy in copies:
        copy.start()
    rows = TILE // heads
    row = lax.broadcasted_iota(jnp.int32, (TILE, TILE), 0)
    col = lax.broadcasted_iota(jnp.int32, (TILE, TILE), 1)
    order = jnp.where(col == (row % rows) * heads + row // rows, 1.0, 0.0).astype(BF)
    table = table_ref[...]
    seen = jnp.concatenate([closure_ref[...]] * per, axis=1) > 0.5
    for t in range(pieces):
        if t * TILE == early:
            grad_copy.wait()
        source, at = (early_ref, t * TILE) if t * TILE < early else (late_ref, t * TILE - early)
        chunk = dot(order, source[at : at + TILE, :], NN).astype(BF)
        for h in range(heads):
            sorted_ref[pl.ds(h * BS + t * rows, rows), :] = chunk[h * rows : (h + 1) * rows]
    for copy in copies:
        copy.wait()
    for h in range(heads):
        tail = pl.ds(h * WIDTH + LAT, ROPE)
        query_ref[tail, :] = turn(query_ref[tail, :].astype(F32), table).astype(BF)
    for t in range(pieces):
        here = pl.ds(t * TILE, TILE)
        score = dot(keys_ref[...], heads_of(query_ref, per * t, per), NN)
        score = jnp.where(seen, score * exponent_scale, MASKED)
        slope = dot(keys_ref[:, :LAT], sorted_ref[here, :], NT)
        expo_ref[:, here] = partial_softmax(score, slope, stat_ref, 0, here)
        slope_ref[:, here] = slope


def key_grads(rows, weight_ref, dscore_ref, query_ref, sorted_ref):
    heads = query_ref.shape[0] // WIDTH
    turned = dot(dscore_ref[rows, :], heads_of(query_ref, 0, heads), NT) * score_scale
    plain = dot(weight_ref[rows, :], sorted_ref[...], NN)
    return turned[:, :LAT] + plain, turned[:, LAT:]


def has_earlier():
    return lax.axis_index("cp") > 0


def mine_kernel(query_ref, sorted_ref, mine_ref, expo_ref, slope_ref, stat_ref):
    per = TILE // BS

    @pl.when(has_earlier())
    def _():
        for t in range(sorted_ref.shape[0] // TILE):
            here = pl.ds(t * TILE, TILE)
            score = dot(mine_ref[...], heads_of(query_ref, per * t, per), NN) * exponent_scale
            slope = dot(mine_ref[:, :LAT], sorted_ref[here, :], NT)
            slope_ref[:, here] = slope
            expo_ref[:BS, here] = partial_softmax(score[:BS], slope[:BS], stat_ref, 0, here)
            expo_ref[BS:, here] = partial_softmax(score[BS:], slope[BS:], stat_ref, 3, here)


def main_kernel(bias_ref, query_ref, sorted_ref, other_ref, own_expo, own_slope, own_stat, mine_expo, mine_slope, mine_stat,
                weight_ref, dscore_ref, gother_ref, score_ref, slope_ref):
    tiles = sorted_ref.shape[0] // TILE
    per = TILE // BS
    whole_mine, part, whole_other, _ = (bias_ref[k : k + 1, :] for k in range(4))

    def products(t):
        here = pl.ds(t * TILE, TILE)
        score_ref[t % 2] = dot(other_ref[...], heads_of(query_ref, per * t, per), NN) * exponent_scale
        slope_ref[t % 2] = dot(other_ref[:, :LAT], sorted_ref[here, :], NT)

    def softmax(t, remote):
        here = pl.ds(t * TILE, TILE)
        before = (
            (own_expo[:, here], own_slope[:, here], own_stat, 0, 0.0),
            (mine_expo[:BS, here], mine_slope[:BS, here], mine_stat, 0, whole_mine),
            (mine_expo[BS:, here], mine_slope[BS:, here], mine_stat, 3, part),
        )
        places = (
            (score_ref[t % 2, :BS], slope_ref[t % 2, :BS], whole_other),
            (score_ref[t % 2, BS:], slope_ref[t % 2, BS:], part),
        )
        if not remote:
            before, places = before[:1], ()
        tops = [stat[k : k + 1, here] + b for _, _, stat, k, b in before]
        largest = functools.reduce(
            jnp.maximum, tops + [jnp.max(s, axis=0, keepdims=True) + b for s, _, b in places]
        )
        factors = [jnp.exp2(top - largest) for top in tops]
        expos = [jnp.exp2(s - (largest - b)) for s, _, b in places]
        inverse = 1.0 / (
            sum(stat[k + 1 : k + 2, here] * f for (_, _, stat, k, _), f in zip(before, factors))
            + sum(jnp.sum(e, axis=0, keepdims=True) for e in expos)
        )
        delta = inverse * (
            sum(stat[k + 2 : k + 3, here] * f for (_, _, stat, k, _), f in zip(before, factors))
            + sum(jnp.sum(e * l, axis=0, keepdims=True) for e, (_, l, _) in zip(expos, places))
        )
        parts = [(e, l, f * inverse) for (e, l, _, _, _), f in zip(before, factors)]
        parts += [(e, l, inverse) for e, (_, l, _) in zip(expos, places)]
        at = 0
        for e, l, factor in parts:
            rows = pl.ds(at, e.shape[0])
            weight = e * factor
            weight_ref[rows, here] = weight.astype(BF)
            dscore_ref[rows, here] = (weight * (l - delta)).astype(BF)
            at += e.shape[0]

    @pl.when(has_earlier())
    def _():
        products(0)
        for t in range(tiles):
            if t + 1 < tiles:
                products(t + 1)
            softmax(t, True)
        lead, tail = key_grads(pl.ds(BS + SIDE, SIDE), weight_ref, dscore_ref, query_ref, sorted_ref)
        gother_ref[:, :LAT] = lead.astype(BF)
        gother_ref[:, LAT:] = tail.astype(BF)

    @pl.when(jnp.logical_not(has_earlier()))
    def _():
        for t in range(tiles):
            softmax(t, False)
        weight_ref[BS:, :] = jnp.zeros((REMOTE, weight_ref.shape[1]), BF)
        dscore_ref[BS:, :] = jnp.zeros((REMOTE, dscore_ref.shape[1]), BF)
        gother_ref[...] = jnp.zeros_like(gother_ref)


def mine_grads_kernel(weight_ref, dscore_ref, query_ref, sorted_ref, out_ref):
    @pl.when(has_earlier())
    def _():
        grads_kernel(slice(BS, BS + SIDE), weight_ref, dscore_ref, query_ref, sorted_ref, out_ref)

    @pl.when(jnp.logical_not(has_earlier()))
    def _():
        out_ref[...] = jnp.zeros_like(out_ref)


def grads_kernel(rows, weight_ref, dscore_ref, query_ref, sorted_ref, out_ref):
    lead, tail = key_grads(rows, weight_ref, dscore_ref, query_ref, sorted_ref)
    out_ref[:, :LAT] = lead
    out_ref[:, LAT:] = tail


def query_kernel(dscore_ref, keys_ref, mine_ref, other_ref, table_ref, dquery_ref, every_ref, turned_ref):
    t = pl.program_id(0)

    @pl.when(t == 0)
    def _():
        every_ref[:BS, :] = keys_ref[...]
        every_ref[BS : BS + SIDE, :] = mine_ref[...]
        every_ref[BS + SIDE :, :] = other_ref[...]
        for lo in range(0, KEYS, BS):
            turned_ref[:, lo : lo + BS] = every_ref[lo : lo + BS, :].T

    dscore = dscore_ref[:, pl.ds(pl.multiple_of(t * STEP, STEP), STEP)]
    grads = dot(turned_ref[...], dscore, NN) * score_scale
    for k in range(STEP // BS):
        part = grads[:, k * BS : (k + 1) * BS]
        dquery_ref[k, :LAT, :] = part[:LAT].astype(BF)
        dquery_ref[k, LAT:, :] = turn_back(part[LAT:], table_ref[...]).astype(BF)


def own_half():
    return pl.ds(pl.multiple_of(this_core() * HALF, HALF), HALF)


def other_half():
    return pl.ds(pl.multiple_of((1 - this_core()) * HALF, HALF), HALF)


def device_kernel(gown_ref, back_ref, half_ref, out_ref, sum_ref):
    sum_ref[...] = gown_ref[...] + back_ref[...].astype(F32)
    sum_ref[own_half(), :] += half_ref[...].astype(F32)
    out_ref[...] = sum_ref[...].astype(BF)


def chip_kernel(device_ref, other_ref, chip_ref, half_ref):
    chip_ref[...] = (device_ref[...].astype(F32) + other_ref[...].astype(F32)).astype(BF)
    half_ref[...] = chip_ref[own_half(), :]


def finish_kernel(chip_ref, near_ref, far_ref, rest_ref, table_ref, out_ref, sum_ref):
    sum_ref[...] = chip_ref[...].astype(F32)
    sum_ref[own_half(), :] += far_ref[...].astype(F32)
    sum_ref[other_half(), :] += rest_ref[BS:, :].astype(F32)
    sum_ref[...] += near_ref[...].astype(F32) + rest_ref[:BS, :].astype(F32)
    for lo in range(0, LAT, BS):
        out_ref[lo : lo + BS, :] = sum_ref[:, lo : lo + BS].astype(BF).T
    out_ref[LAT:, :] = turn_back(sum_ref[:, LAT:].T, table_ref[...]).astype(BF)


def by_core(block, even, odd):
    tp, cp = lax.axis_size("tp"), lax.axis_size("cp")
    route = []
    for t in range(tp):
        step = odd if t % 2 else even
        for c in range(cp):
            if 0 <= c + step < cp or WRAP:
                route.append((t * cp + c, t * cp + (c + step) % cp))
    return lax.ppermute(block, ("tp", "cp"), route)


WRAP = True


def other_core(block):
    return lax.ppermute(block, "tp", [(t, t ^ 1) for t in range(lax.axis_size("tp"))])


def along_x(block, even, odd):
    route = [(t, t ^ (2 * (odd if t % 2 else even))) for t in range(lax.axis_size("tp"))]
    return lax.ppermute(block, "tp", route)


def on_device(query, latent, grad_out, ancestors, parents):
    rows, heads, _ = query.shape
    total = rows * heads
    half = ROPE // 2
    lane_freq = rope_base ** (-2.0 * np.arange(half, dtype=np.float64) / ROPE)
    freq = jnp.asarray(np.tile(lane_freq[:, None], (1, BS)), dtype=F32)
    params = pltpu.CompilerParams(vmem_limit_bytes=16 * 2**20)
    outside = pl.BlockSpec(memory_space=pltpu.HBM)

    def call(kernel, name, ins, outs, flops=0, **more):
        return pl.pallas_call(
            kernel,
            in_specs=ins,
            out_specs=[whole()] * len(outs),
            out_shape=[vmem(*o) for o in outs],
            cost_estimate=pl.CostEstimate(flops=flops, bytes_accessed=4 * total * WIDTH, transcendentals=0),
            compiler_params=params,
            name=name,
            **more,
        )

    keys, keys_half, table, closure, bias, early = call(
        keys_kernel,
        "keys",
        [scalars(), whole(), outside, outside, outside],
        [((BS, WIDTH), BF), ((HALF, WIDTH), BF), ((ROPE, BS), F32), ((BS, BS), F32), ((8, TILE), F32), ((total // 4, LAT), BF)],
        scratch_shapes=[pltpu.VMEM((half, BS), F32), pltpu.VMEM((WIDTH, BS), BF), pltpu.SemaphoreType.DMA((3,))],
    )(*map(in_hbm, (ancestors, parents.reshape(1, BS), freq, latent.T, grad_out.reshape(total, LAT))))

    fetched = by_core(keys, EVEN, ODD)
    fetched_half = by_core(keys_half, BOTH, BOTH)

    q, g, own_expo, own_slope, own_stat = call(
        functools.partial(own_kernel, heads),
        "own",
        [outside] * 2 + [whole()] * 4,
        [((heads * WIDTH, rows), BF), ((total, LAT), BF), ((BS, total), F32), ((BS, total), F32), ((8, total), F32)],
        flops=2 * total * BS * 1800,
        scratch_shapes=[pltpu.VMEM((total - total // 4, LAT), BF), pltpu.SemaphoreType.DMA((total // TILE + 1,))],
    )(in_hbm(query.transpose(1, 2, 0).reshape(heads * WIDTH, rows)), in_hbm(grad_out.reshape(total, LAT)),
      early, keys, table, closure)

    mine, q = lax.optimization_barrier((jnp.concatenate([fetched, fetched_half]), q))
    other = other_core(mine)
    mine_expo, mine_slope, mine_stat = call(
        mine_kernel,
        "mine",
        [whole()] * 3,
        [((SIDE, total), F32), ((SIDE, total), F32), ((8, total), F32)],
        flops=2 * total * SIDE * 1280,
    )(q, g, mine)

    weight, dscore, gother = call(
        main_kernel,
        "main",
        [whole()] * 10,
        [((KEYS, total), BF), ((KEYS, total), BF), ((SIDE, WIDTH), BF)],
        flops=2 * total * SIDE * 2560,
        scratch_shapes=[pltpu.VMEM((2, SIDE, TILE), F32), pltpu.VMEM((2, SIDE, TILE), F32)],
    )(bias, q, g, other, own_expo, own_slope, own_stat, mine_expo, mine_slope, mine_stat)

    gother = other_core(gother)
    (gmine,) = call(
        mine_grads_kernel,
        "grads",
        [whole()] * 4,
        [((SIDE, WIDTH), F32)],
        flops=2 * total * SIDE * 1280,
    )(weight, dscore, q, g)
    gmine = (gmine + gother.astype(F32)).astype(BF)
    back = by_core(gmine[:BS], -EVEN, -ODD)
    back_half = by_core(gmine[BS:], -BOTH, -BOTH)

    (gown,) = call(
        functools.partial(grads_kernel, slice(0, BS)),
        "gown",
        [whole()] * 4,
        [((BS, WIDTH), F32)],
        flops=2 * total * BS * 1280,
    )(weight, dscore, q, g)
    (device_sum,) = call(
        device_kernel,
        "device",
        [whole()] * 3,
        [((BS, WIDTH), BF)],
        scratch_shapes=[pltpu.VMEM((BS, WIDTH), F32)],
    )(gown, back, back_half)
    chip_sum, chip_half = call(
        chip_kernel, "chip", [whole()] * 2, [((BS, WIDTH), BF), ((HALF, WIDTH), BF)]
    )(device_sum, other_core(device_sum))
    chip_sum, dscore = lax.optimization_barrier((chip_sum, dscore))
    near = along_x(chip_sum, 1, 3)
    far = along_x(chip_half, 2, 2)
    dquery = pl.pallas_call(
        query_kernel,
        grid=(total // STEP,),
        in_specs=[whole()] * 5,
        out_specs=pl.BlockSpec((STEP // BS, WIDTH, BS), lambda t: (t, 0, 0)),
        out_shape=jax.ShapeDtypeStruct((heads, WIDTH, rows), BF),
        scratch_shapes=[pltpu.VMEM((KEYS, WIDTH), BF), pltpu.VMEM((WIDTH, KEYS), BF)],
        cost_estimate=pl.CostEstimate(flops=2 * total * KEYS * 768, bytes_accessed=4 * total * WIDTH, transcendentals=0),
        compiler_params=params,
        name="dquery",
    )(dscore, keys, mine, other, table)
    near, dquery = lax.optimization_barrier((near, dquery))
    rest = other_core(jnp.concatenate([near, far]))
    d_latent = pl.pallas_call(
        finish_kernel,
        in_specs=[whole()] * 5,
        out_specs=whole(),
        out_shape=jax.ShapeDtypeStruct((WIDTH, BS), BF),
        scratch_shapes=[pltpu.VMEM((BS, WIDTH), F32)],
        compiler_params=params,
        name="finish",
    )(*map(in_vmem, (chip_sum, near, far, rest, table)))
    return (dquery.transpose(2, 0, 1), d_latent.T)


def solution(mesh):
    placed = (P("cp", "tp", None), P("cp", None), P("cp", "tp", None), P("cp", None), P("cp"))
    return jax.shard_map(
        on_device,
        mesh=mesh,
        in_specs=placed,
        out_specs=(P("cp", "tp", None), P("cp", None)),
        check_vma=False,
    )
```
